512 devices in a mesh: layer: 8 (over z_hi, x), row: 8 (over z_lo), col: 8 (over y, core).
Axes of the slice: x: 4, y: 4, z: 16 (z_hi: 2, z_lo: 8; z = z_hi * 8 + z_lo), core: 2. Of those that a mesh axis runs over, the one named last changes fastest.
Arguments:
- covariance: float32 [65536, 8192], P(('layer', 'row'), 'col'), parts along dimension 0, may hold values from -2 to 20, as said below
- weight: bfloat16 [65536, 2, 1024], P(('layer', 'col', 'row')), parts along dimension 0, may hold values from -6 to 6
- factor_a: bfloat16 [65536, 2, 256], P(('layer', 'col', 'row')), parts along dimension 0, may hold values from -1.5 to 1.5
- factor_b: bfloat16 [16, 256, 1024], P('layer', ('row', 'col')), parts along dimension 0, may hold values from -1.5 to 1.5
Outputs:
- new_a: float32 [65536, 2, 256], P(('layer', 'col', 'row')), parts along dimension 0
- new_b: float32 [16, 256, 1024], P('layer', ('row', 'col')), parts along dimension 0
The draws below stay inside these ranges and needn't reach their ends.
There are 8 independent parts, one for each index of `layer`. The reference program is written for one: setup_inputs(seed, part) draws one part's arguments, and reference() takes and returns one part's arrays. A program takes and returns all parts, laid end to end along the dimension named above; each array names one. Nothing has to cross between parts.
Inputs may be any that keep to these rules, and one draw needn't show every extreme that they name: covariance is symmetric and positive definite.
All inputs are finite; a program needn't handle non-finite values.
Results may differ from the reference program's by a relative error of at most 0.0012.
Values may be sent and summed in bfloat16 or wider, within the bound.
A program may use at most 64 MiB of HBM per device.

```python
import math
import jax
import jax.numpy as jnp
from jax import lax

D = 8192
O = 1024
R = 256


def draw_covariance(key, part):
    key_noise = jax.random.fold_in(key, 11)
    key_scale = jax.random.fold_in(key, 23)
    entries = jax.random.normal(key_noise, (D, D), jnp.float32)
    symmetric = (entries + entries.T) * (0.35 / math.sqrt(2.0 * D)) + jnp.eye(D, dtype=jnp.float32)
    upper_log = math.log(2.0)
    scales = jnp.exp(jax.random.uniform(key_scale, (D,), jnp.float32, math.log(0.5), upper_log))
    return scales[:, None] * symmetric * scales[None, :]


def block_levels(own_key, shape, shards, low, high):
    gain = 1.0
    for axis_at, shards_of in shards:
        draws = jax.random.uniform(jax.random.fold_in(jax.random.fold_in(own_key, 6), axis_at), (shards_of,), jnp.float32, low / len(shards), high / len(shards))
        gain = gain * jnp.repeat(jnp.exp(draws), shape[axis_at] // shards_of).reshape((-1,) + (1,) * (len(shape) - 1 - axis_at))
    return gain


def bell_draw(stream_key, extent, deviation, reach, pieces=(), kind=jnp.bfloat16):
    level = block_levels(stream_key, extent, pieces, -0.22, 0.18) if pieces else 1.0
    result = jax.random.normal(stream_key, extent, jnp.float32) * deviation * level
    return jnp.minimum(jnp.maximum(result, -reach), reach).astype(kind)


def setup_inputs(seed: int = 0, part: int = 0) -> dict:
    keys = jax.random.split(jax.random.key(seed), 5)
    part_splits = jax.random.split(jax.random.fold_in(keys[4], part), 5)
    covariance = draw_covariance(jax.random.fold_in(jax.random.fold_in(keys[4], part), 71), part)
    weight = bell_draw(part_splits[1], (D, 2, O), 1.0, 6.0, ((0, 64),))
    factor_a = bell_draw(part_splits[2], (D, 2, R), 0.25, 1.5, ((0, 64),))
    factor_b = bell_draw(part_splits[3], (2, R, O), 0.25, 1.5, ((1, 64),))
    return dict(covariance=covariance, weight=weight, factor_a=factor_a, factor_b=factor_b)


def reference(covariance, weight, factor_a, factor_b):
    highest = lax.Precision.HIGHEST
    right_f = factor_b.astype(jnp.float32)
    left_f = factor_a.astype(jnp.float32)
    diff_one = (weight.astype(jnp.float32) - jnp.einsum("nkr,kro->nko", left_f, right_f, precision=highest)).astype(jnp.bfloat16)
    proj_one = jnp.einsum("nko,kro->nkr", diff_one.astype(jnp.float32), right_f, precision=highest)
    grad_one = jnp.dot(covariance, proj_one.reshape(D, 2 * R), precision=highest, preferred_element_type=jnp.float32)
    new_a = left_f + (4.0 / O) * grad_one.reshape(D, 2, R)
    diff_two = (weight.astype(jnp.float32) - jnp.einsum("nkr,kro->nko", new_a, right_f, precision=highest)).astype(jnp.bfloat16)
    field = jnp.dot(covariance, new_a.reshape(D, 2 * R), precision=highest, preferred_element_type=jnp.float32)
    grad_two = jnp.einsum("nkr,nko->kro", field.reshape(D, 2, R), diff_two.astype(jnp.float32), precision=highest)
    new_b = right_f + (8.0 / D) * grad_two
    return new_a, new_b
```

```python
import functools

import jax
import jax.numpy as jnp
from jax import lax
from jax.experimental import pallas as pl
from jax.experimental.pallas import tpu as pltpu
from jax.sharding import PartitionSpec as P

MESH = pl.DeviceIdType.MESH
F32 = jnp.float32
BF = jnp.bfloat16
D = 8192
O = 1024
R = 256
C2 = 2 * R
FIELD_DOWN = 1.0 / 256.0
FIELD_UP = 256.0

NN = (((1,), (0,)), ((), ()))
NT = (((1,), (1,)), ((), ()))


def enc(x):
    s = x * x
    s = s * s
    return jnp.where(x < 0, -s, s).astype(BF)


def dec(v):
    f = v.astype(F32)
    r = jnp.sqrt(jnp.sqrt(jnp.abs(f)))
    return jnp.where(f < 0, -r, r)


def split(x):
    hi = x.astype(BF)
    return hi, (x - hi.astype(F32)).astype(BF)


def dot(a, b, dims=NN):
    return lax.dot_general(a, b, dims, preferred_element_type=F32)


def source_column(i):
    core = i >> 8
    y = (i >> 6) & 3
    z = (i >> 3) & 7
    k = (i >> 2) & 1
    return k * R + 4 * (z * 8 + y * 2 + core) + (i & 3)


def kernel(
    cov_hbm, w_ref, a_ref, bs_ref, bown_ref, na_ref, nb_ref,
    cov, chi, clo, gat, ball, aint, xg, xh, xl, fas, fag, pb, pes, per_, ses, ser,
    nag, tz, tn, fb, zs, zr, d2, p2, fcs, fcr, fys, fyr, fsum, fzs, fzr,
    cov_sem, bz_s, bz_r, by_s, by_r, bc_s, bc_r, fa_s, fa_r, xg_s, xg_r, pc_s, pc_r, ps_s, ps_r,
    ny_s, nc_s, ng_r, tz_s, tz_r, tn_s, tn_r, zr_s, zr_r, fc_s, fc_r, fy_s, fy_r, fz_s, fz_r,
):
    layer = lax.axis_index("layer")
    z = lax.axis_index("row")
    c = lax.axis_index("col")
    y = lax.div(c, 2)
    core = lax.rem(c, 2)
    other = c + 1 - 2 * core

    def rc(src, dst, ss, rs, zz, cc):
        return pltpu.make_async_remote_copy(
            src_ref=src, dst_ref=dst, send_sem=ss, recv_sem=rs,
            device_id=(layer, zz, cc), device_id_type=MESH,
        )

    cov_copy = pltpu.make_async_copy(cov_hbm, cov, cov_sem)
    cov_copy.start()

    barrier = pltpu.get_barrier_semaphore()
    for d in range(1, 8):
        pl.semaphore_signal(barrier, inc=1, device_id=(layer, lax.rem(z + d, 8), c), device_id_type=MESH)
        pl.semaphore_signal(barrier, inc=1, device_id=(layer, z, lax.rem(c + d, 8)), device_id_type=MESH)
    pl.semaphore_wait(barrier, 14)

    gat[core, y, z] = bs_ref[...]
    zpeer = [lax.rem(z + d, 8) for d in range(1, 8)]
    ypeer = [lax.rem(y + d, 4) for d in range(1, 4)]

    def b_z(zz):
        return rc(gat.at[core, y, z], gat.at[core, y, z], bz_s.at[zz], bz_r.at[z], zz, c)

    def b_z_in(zz):
        return rc(gat.at[core, y, zz], gat.at[core, y, zz], bz_s.at[zz], bz_r.at[zz], zz, c)

    def b_y(yy):
        return rc(gat.at[core, y], gat.at[core, y], by_s.at[yy], by_r.at[y], z, 2 * yy + core)

    def b_y_in(yy):
        return rc(gat.at[core, yy], gat.at[core, yy], by_s.at[yy], by_r.at[yy], z, 2 * yy + core)

    def b_c(yy):
        return rc(gat.at[core, yy], gat.at[core, yy], bc_s.at[yy], bc_r.at[yy], z, other)

    def b_c_in(yy):
        return rc(gat.at[1 - core, yy], gat.at[1 - core, yy], bc_s.at[yy], bc_r.at[yy], z, other)

    for zz in zpeer:
        b_z(zz).start()

    shape_sq = (C2, C2)
    unmix = (lax.broadcasted_iota(jnp.int32, shape_sq, 0) == source_column(lax.broadcasted_iota(jnp.int32, shape_sq, 1))).astype(F32).astype(BF)
    unmix_t = (lax.broadcasted_iota(jnp.int32, shape_sq, 1) == source_column(lax.broadcasted_iota(jnp.int32, shape_sq, 0))).astype(F32).astype(BF)
    aint[...] = dot(a_ref[...], unmix).astype(BF)
    fas[...] = dot(unmix_t, a_ref[...], NT).astype(BF)

    def f_a():
        return rc(fas, fag.at[z], fa_s.at[0], fa_r.at[z], c, c)

    def f_a_in(zz):
        return rc(fas, fag.at[zz], fa_s.at[0], fa_r.at[zz], c, c)

    pl.when(z != c)(lambda: f_a().start())

    cov_copy.wait()

    @pl.loop(0, 8)
    def _(i):
        rows = pl.ds(pl.multiple_of(i * 128, 128), 128)
        hi, lo = split(cov[rows, :])
        chi[rows, :] = hi
        clo[rows, :] = lo

    for zz in zpeer:
        b_z_in(zz).wait_recv()
    for yy in ypeer:
        b_y(yy).start()
    b_c(y).start()

    row_i = lax.broadcasted_iota(jnp.int32, (128, 128), 0)
    col_i = lax.broadcasted_iota(jnp.int32, (128, 128), 1)
    pick = (col_i == 2 * (row_i & 63) + (row_i >> 6)).astype(F32).astype(BF)

    def unpack(cc, yy):
        both = dot(pick, gat[cc, yy].reshape(128, 512)).astype(BF)
        rows = pl.ds(pl.multiple_of((cc * 4 + yy) * 64, 64), 64)
        ball[rows, 0:512] = both[0:64]
        ball[rows, 512:1024] = both[64:128]

    unpack(core, y)
    for yy in ypeer:
        b_y_in(yy).wait_recv()
        b_c(yy).start()
        unpack(core, yy)
    b_c_in(y).wait_recv()
    unpack(1 - core, y)
    for yy in ypeer:
        b_c_in(yy).wait_recv()
        unpack(1 - core, yy)

    lane_k = (lax.broadcasted_iota(jnp.int32, (128, C2), 1) >> 2) & 1
    sub_k = (lax.broadcasted_iota(jnp.int32, (C2, 128), 0) >> 2) & 1

    proj = None
    for k in range(2):
        a_k = jnp.where(lane_k == k, aint[...].astype(F32), 0.0).astype(BF)
        diff = (w_ref[:, k * O:(k + 1) * O].astype(F32) - dot(a_k, ball[...])).astype(BF)
        part = dot(ball[...], diff, NT)
        proj = part if k == 0 else jnp.where(sub_k == 1, part, proj)
    own = enc(proj)
    xg[z] = own

    def x_out(direction, s, q, zz):
        piece = xg.at[s, pl.ds(q * 128, 128)]
        return rc(piece, piece, xg_s.at[direction, s, q], xg_r.at[s, q], zz, c)

    up, down = lax.rem(z + 1, 8), lax.rem(z + 7, 8)
    for q in range(4):
        pl.when(z < 7)(lambda: x_out(0, z, q, up).start())
        pl.when(z > 0)(lambda: x_out(1, z, q, down).start())

    def x_decode(s):
        lanes = pl.ds(pl.multiple_of(s * 128, 128), 128)
        hi, lo = split(dec(xg[s]))
        xh[:, lanes] = hi
        xl[:, lanes] = lo

    x_decode(z)

    @pl.when(z != c)
    def _():
        @pl.loop(0, 8)
        def _(j):
            pb[j] = jnp.zeros((C2, 128), F32)

    @pl.when(z == c)
    def _():
        fag[z] = fas[...]
        for zz in zpeer:
            f_a_in(zz).wait_recv()

        @pl.loop(0, 8)
        def _(j):
            pb[j] = fag[j].astype(F32)

    @pl.loop(1, 8)
    def _(t):
        lo_s, hi_s = z - t, z + t
        for q in range(4):
            @pl.when(lo_s >= 0)
            def _():
                x_out(0, lo_s, q, up).wait_recv()
                pl.when(z < 7)(lambda: x_out(0, lo_s, q, up).start())

            @pl.when(hi_s <= 7)
            def _():
                x_out(1, hi_s, q, down).wait_recv()
                pl.when(z > 0)(lambda: x_out(1, hi_s, q, down).start())

        pl.when(lo_s >= 0)(lambda: x_decode(lo_s))
        pl.when(hi_s <= 7)(lambda: x_decode(hi_s))

    def p_c(yy):
        return rc(pes.at[yy], per_.at[yy], pc_s.at[yy], pc_r.at[yy], z, other)

    def p_y(yy):
        return rc(ses.at[yy], ser.at[y], ps_s.at[yy], ps_r.at[y], z, 2 * yy + core)

    def p_y_in(yy):
        return rc(ses.at[yy], ser.at[yy], ps_s.at[yy], ps_r.at[yy], z, 2 * yy + core)

    @pl.loop(0, 4)
    def _(d):
        yy = lax.rem(y + 1 + d, 4)
        rows = pl.ds(pl.multiple_of(yy * 256, 256), 256)
        c_hi = chi[rows, :]
        total = dot(xh[...], c_hi, NT) + dot(xl[...], c_hi, NT) + dot(xh[...], clo[rows, :], NT)
        total = total * (4.0 / O)
        pb[2 * yy] = pb[2 * yy] + total[:, 0:128]
        pb[2 * yy + 1] = pb[2 * yy + 1] + total[:, 128:256]
        pes[yy] = enc(pb[2 * yy + 1 - core])
        p_c(yy).start()

    for yy in ypeer:
        p_c(yy).wait_recv()
        ses[yy] = enc(pb[2 * yy + core] + dec(per_[yy]))
        p_y(yy).start()
    p_c(y).wait_recv()
    new_a = pb[c] + dec(per_[y])
    for yy in ypeer:
        p_y_in(yy).wait_recv()
        new_a = new_a + dec(ser[yy])
    nag[c] = enc(new_a).reshape(8, 64, 128)

    def n_y(yy):
        return rc(nag.at[c], nag.at[c], ny_s.at[yy], ng_r.at[c], z, 2 * yy + core)

    def n_c(yy):
        piece = nag.at[2 * yy + core]
        return rc(piece, piece, nc_s.at[yy], ng_r.at[2 * yy + core], z, other)

    def n_in(j):
        return rc(nag.at[j], nag.at[j], nc_s.at[0], ng_r.at[j], z, other)

    for yy in ypeer:
        n_y(yy).start()
    n_c(y).start()

    def n_decode(j):
        lanes = pl.ds(pl.multiple_of(j * 128, 128), 128)
        hi, lo = split(dec(nag[j].reshape(C2, 128)))
        xh[:, lanes] = hi
        xl[:, lanes] = lo

    n_decode(c)
    for yy in ypeer:
        n_in(2 * yy + core).wait_recv()
        n_c(yy).start()
        n_decode(2 * yy + core)
    n_in(2 * y + 1 - core).wait_recv()
    n_decode(2 * y + 1 - core)
    for yy in ypeer:
        n_in(2 * yy + 1 - core).wait_recv()
        n_decode(2 * yy + 1 - core)

    def t_z(zz):
        return rc(nag.at[zz, c], tz.at[z], tz_s.at[zz], tz_r.at[z], zz, c)

    def t_z_in(zz):
        return rc(nag.at[zz, c], tz.at[zz], tz_s.at[zz], tz_r.at[zz], zz, c)

    def t_n(r):
        return rc(tz.at[r], tn.at[c], tn_s.at[r], tn_r.at[c], z, r)

    def t_n_in(r):
        return rc(tz.at[r], tn.at[r], tn_s.at[r], tn_r.at[r], z, r)

    cpeer = [lax.rem(c + d, 8) for d in range(1, 8)]
    for zz in zpeer:
        t_z(zz).start()
    tz[z] = nag[z, c]

    @pl.loop(0, 4)
    def _(i):
        lanes = pl.ds(pl.multiple_of(i * 256, 256), 256)
        c_hi = chi[:, lanes]
        total = dot(xh[...], c_hi) + dot(xl[...], c_hi) + dot(xh[...], clo[:, lanes])
        total = total * FIELD_DOWN
        fb[2 * i] = total[:, 0:128]
        fb[2 * i + 1] = total[:, 128:256]

    def z_out(direction, dest, q, zz):
        rows = pl.ds(q * 128, 128)
        return rc(
            zs.at[direction, dest, rows], zr.at[direction, dest, rows],
            zr_s.at[direction, dest, q], zr_r.at[direction, dest, q], zz, c,
        )

    def z_step(direction, dest, first, last, zz):
        for q in range(4):
            rows = pl.ds(q * 128, 128)

            @pl.when(jnp.logical_not(first))
            def _():
                z_out(direction, dest, q, zz).wait_recv()
                fb[dest, rows] = fb[dest, rows] + dec(zr[direction, dest, rows])

            @pl.when(jnp.logical_not(last))
            def _():
                zs[direction, dest, rows] = enc(fb[dest, rows])
                z_out(direction, dest, q, zz).start()

    @pl.loop(0, 8)
    def _(t):
        @pl.when(t >= z)
        def _():
            z_step(0, 7 + z - t, z == 0, t == 7, up)

        @pl.when(t >= 7 - z)
        def _():
            z_step(1, t - 7 + z, z == 7, t == 7, down)

        @pl.when(t == 3)
        def _():
            for zz in zpeer:
                t_z_in(zz).wait_recv()
            for r in cpeer:
                t_n(r).start()
            tn[c] = tz[c]

        @pl.when(t == 6)
        def _():
            for r in cpeer:
                t_n_in(r).wait_recv()
            rows_a = dec(tn[...].reshape(C2, 128)).T
            hi, lo = split(rows_a)
            lo2 = (rows_a - hi.astype(F32) - lo.astype(F32)).astype(BF)
            back = (lax.broadcasted_iota(jnp.int32, shape_sq, 0) == source_column(lax.broadcasted_iota(jnp.int32, shape_sq, 1))).astype(F32).astype(BF)
            na_ref[...] = dot(hi, back, NT) + dot(lo, back, NT) + dot(lo2, back, NT)
            for k in range(2):
                hi_k = jnp.where(lane_k == k, hi.astype(F32), 0.0).astype(BF)
                lo_k = jnp.where(lane_k == k, lo.astype(F32), 0.0).astype(BF)
                fit = dot(hi_k, ball[...]) + dot(lo_k, ball[...])
                d2[k * 128:(k + 1) * 128, :] = (w_ref[:, k * O:(k + 1) * O].astype(F32) - fit).astype(BF)

    field = fb[z] * (FIELD_UP * 8.0 / D)
    wide = jnp.concatenate([jnp.where(sub_k == 0, field, 0.0), jnp.where(sub_k == 1, field, 0.0)], axis=1)
    hi, lo = split(wide)
    xh[:, 0:256] = hi
    xl[:, 0:256] = lo

    def f_c(yy):
        return rc(fcs.at[yy], fcr.at[yy], fc_s.at[yy], fc_r.at[yy], z, other)

    def f_y(yy):
        return rc(fys.at[yy], fyr.at[y], fy_s.at[yy], fy_r.at[y], z, 2 * yy + core)

    def f_y_in(yy):
        return rc(fys.at[yy], fyr.at[yy], fy_s.at[yy], fy_r.at[yy], z, 2 * yy + core)

    def f_z(zz):
        return rc(fzs.at[zz], fzr.at[z], fz_s.at[zz], fz_r.at[z], zz, c)

    def f_z_in(zz):
        return rc(fzs.at[zz], fzr.at[zz], fz_s.at[zz], fz_r.at[zz], zz, c)

    def half(which):
        rows = pl.ds(pl.multiple_of(which * 256, 256), 256)
        return dot(xh[rows, 0:256], d2[...]) + dot(xl[rows, 0:256], d2[...])

    fcs[...] = enc(half(1 - core)).reshape(4, 64, O)
    for yy in ypeer + [y]:
        f_c(yy).start()
    p2[...] = half(core).reshape(4, 64, O)
    for yy in ypeer:
        f_c(yy).wait_recv()
        fys[yy] = enc(p2[yy] + dec(fcr[yy]))
        f_y(yy).start()
    f_c(y).wait_recv()
    total = p2[y] + dec(fcr[y])
    for yy in ypeer:
        f_y_in(yy).wait_recv()
        total = total + dec(fyr[yy])
    fsum[...] = total.reshape(8, 8, O)
    for zz in zpeer:
        mine = fsum[zz]
        fzs[zz] = enc(jnp.concatenate([mine[:, 0:512], mine[:, 512:1024]], axis=0))
        f_z(zz).start()
    rest = None
    for zz in zpeer:
        f_z_in(zz).wait_recv()
        got = dec(fzr[zz])
        rest = got if rest is None else rest + got
    nb_ref[...] = bown_ref[...] + fsum[z] + jnp.concatenate([rest[0:8], rest[8:16]], axis=1)

    for zz in zpeer:
        b_z(zz).wait_send()
        t_z(zz).wait_send()
        f_z(zz).wait_send()
    for r in cpeer:
        t_n(r).wait_send()
    for yy in ypeer:
        b_y(yy).wait_send()
        p_y(yy).wait_send()
        n_y(yy).wait_send()
        f_y(yy).wait_send()
    for yy in ypeer + [y]:
        b_c(yy).wait_send()
        p_c(yy).wait_send()
        n_c(yy).wait_send()
        f_c(yy).wait_send()
    pl.when(z != c)(lambda: f_a().wait_send())

    @pl.loop(0, 8)
    def _(s):
        for q in range(4):
            pl.when(jnp.logical_and(s <= z, z < 7))(lambda: x_out(0, s, q, up).wait_send())
            pl.when(jnp.logical_and(s >= z, z > 0))(lambda: x_out(1, s, q, down).wait_send())
            pl.when(s > z)(lambda: z_out(0, s, q, up).wait_send())
            pl.when(s < z)(lambda: z_out(1, s, q, down).wait_send())


def per_device(covariance, weight, factor_a, factor_b):
    n = weight.shape[0]
    vm = pl.BlockSpec(memory_space=pltpu.VMEM)
    blk = (8, C2, 128)
    dma = pltpu.SemaphoreType.DMA
    new_a, new_b = pl.pallas_call(
        kernel,
        name="refine",
        out_shape=(jax.ShapeDtypeStruct((n, C2), F32), jax.ShapeDtypeStruct((8, O), F32)),
        in_specs=[pl.BlockSpec(memory_space=pl.ANY), vm, vm, vm, vm],
        out_specs=(vm, vm),
        scratch_shapes=[
            pltpu.VMEM((1024, 1024), F32),
            pltpu.VMEM((1024, 1024), BF),
            pltpu.VMEM((1024, 1024), BF),
            pltpu.VMEM((2, 4, 8, 16, 512), BF),
            pltpu.VMEM((C2, O), BF),
            pltpu.VMEM((128, C2), BF),
            pltpu.VMEM(blk, BF),
            pltpu.VMEM((C2, 1024), BF),
            pltpu.VMEM((C2, 1024), BF),
            pltpu.VMEM((C2, 128), BF),
            pltpu.VMEM(blk, BF),
            pltpu.VMEM(blk, F32),
            pltpu.VMEM((4, C2, 128), BF),
            pltpu.VMEM((4, C2, 128), BF),
            pltpu.VMEM((4, C2, 128), BF),
            pltpu.VMEM((4, C2, 128), BF),
            pltpu.VMEM((8, 8, 64, 128), BF),
            pltpu.VMEM((8, 64, 128), BF),
            pltpu.VMEM((8, 64, 128), BF),
            pltpu.VMEM(blk, F32),
            pltpu.VMEM((2,) + blk, BF),
            pltpu.VMEM((2,) + blk, BF),
            pltpu.VMEM((256, O), BF),
            pltpu.VMEM((4, 64, O), F32),
            pltpu.VMEM((4, 64, O), BF),
            pltpu.VMEM((4, 64, O), BF),
            pltpu.VMEM((4, 64, O), BF),
            pltpu.VMEM((4, 64, O), BF),
            pltpu.VMEM((8, 8, O), F32),
            pltpu.VMEM((8, 16, 512), BF),
            pltpu.VMEM((8, 16, 512), BF),
            dma,
            dma((8,)), dma((8,)), dma((4,)), dma((4,)), dma((4,)), dma((4,)),
            dma((1,)), dma((8,)),
            dma((2, 8, 4)), dma((8, 4)),
            dma((4,)), dma((4,)), dma((4,)), dma((4,)),
            dma((4,)), dma((4,)), dma((8,)),
            dma((8,)), dma((8,)), dma((8,)), dma((8,)),
            dma((2, 8, 4)), dma((2, 8, 4)),
            dma((4,)), dma((4,)), dma((4,)), dma((4,)), dma((8,)), dma((8,)),
        ],
        compiler_params=pltpu.CompilerParams(
            collective_id=0, has_side_effects=True, vmem_limit_bytes=52 * 2**20
        ),
    )(
        covariance,
        weight.reshape(n, 2 * O),
        factor_a.reshape(n, C2),
        factor_b.reshape(16, 512),
        factor_b.reshape(8, O).astype(F32),
    )
    return new_a.reshape(n, 2, R), new_b.reshape(2, 4, O)


def solution(mesh):
    in_specs = (
        P(("layer", "row"), "col"),
        P(("layer", "col", "row"), None, None),
        P(("layer", "col", "row"), None, None),
        P("layer", ("row", "col"), None),
    )
    out_specs = (P(("layer", "col", "row"), None, None), P("layer", ("row", "col"), None))
    return jax.shard_map(
        per_device, mesh=mesh, in_specs=in_specs, out_specs=out_specs, check_vma=False
    )
```

```python
import functools

import jax
import jax.numpy as jnp
from jax import lax
from jax.experimental import pallas as pl
from jax.experimental.pallas import tpu as pltpu
from jax.sharding import PartitionSpec as P

MESH = pl.DeviceIdType.MESH
F32 = jnp.float32
BF = jnp.bfloat16
D = 8192
O = 1024
R = 256
C2 = 2 * R
FIELD_DOWN = 1.0 / 256.0
FIELD_UP = 256.0

NN = (((1,), (0,)), ((), ()))
NT = (((1,), (1,)), ((), ()))


def enc(x):
    s = x * x
    s = s * s
    return jnp.where(x < 0, -s, s).astype(BF)


def dec(v):
    f = v.astype(F32)
    r = jnp.sqrt(jnp.sqrt(jnp.abs(f)))
    return jnp.where(f < 0, -r, r)


def split(x):
    hi = x.astype(BF)
    return hi, (x - hi.astype(F32)).astype(BF)


def dot(a, b, dims=NN):
    return lax.dot_general(a, b, dims, preferred_element_type=F32)


def source_column(i):
    core = i >> 8
    y = (i >> 6) & 3
    z = (i >> 3) & 7
    k = (i >> 2) & 1
    return k * R + 4 * (z * 8 + y * 2 + core) + (i & 3)


def kernel(
    cov_hbm, w_hbm, a_ref, b_ref, na_ref, nb_ref,
    cov, wv, wk, chi, clo, ccat, gat, ball, aint, xg, xh, xl, fas, fa1, fag, fa3, pb, pes, per_, ses, ser,
    nag, tz, tn, fb, zs, zr, d2, p2, fcs, fcr, fys, fyr, fsum, fzs, fzr,
    cov_sem, w_sem, bz_s, bz_r, by_s, by_r, bc_s, bc_r, f1_s, f1_r, f2_s, f2_r, f3_s, f3_r, xg_s, xg_r,
    pc_s, pc_r, ps_s, ps_r, ny_s, nc_s, ng_r, tz_s, tz_r, tn_s, tn_r, zr_s, zr_r,
    fc_s, fc_r, fy_s, fy_r, fz_s, fz_r,
):
    layer = lax.axis_index("layer")
    z = lax.axis_index("row")
    c = lax.axis_index("col")
    y = lax.div(c, 2)
    core = lax.rem(c, 2)
    other = c + 1 - 2 * core

    def rc(src, dst, ss, rs, zz, cc):
        return pltpu.make_async_remote_copy(
            src_ref=src, dst_ref=dst, send_sem=ss, recv_sem=rs,
            device_id=(layer, zz, cc), device_id_type=MESH,
        )

    cov_copy = pltpu.make_async_copy(cov_hbm, cov, cov_sem)
    w_copy = pltpu.make_async_copy(w_hbm, wv, w_sem)
    cov_copy.start()
    w_copy.start()

    zpeer = [lax.rem(z + d, 8) for d in (1, 7, 2, 6, 3, 5, 4)]
    ypeer = [lax.rem(y + d, 4) for d in (1, 3, 2)]
    cpeer = [lax.rem(c + d, 8) for d in range(1, 8)]

    barrier = pltpu.get_barrier_semaphore()
    for zz in zpeer:
        pl.semaphore_signal(barrier, inc=1, device_id=(layer, zz, c), device_id_type=MESH)
    for cc in cpeer:
        pl.semaphore_signal(barrier, inc=1, device_id=(layer, z, cc), device_id_type=MESH)

    b_own = b_ref[...].astype(F32)
    b_own = jnp.concatenate([b_own[0], b_own[1]], axis=0)
    gat[core, y, z] = jnp.concatenate([b_own[:, 0:512], b_own[:, 512:1024]], axis=0).astype(BF)

    shape_sq = (C2, C2)
    row_sq = lax.broadcasted_iota(jnp.int32, shape_sq, 0)
    col_sq = lax.broadcasted_iota(jnp.int32, shape_sq, 1)
    unmix = (row_sq == source_column(col_sq)).astype(F32).astype(BF)
    unmix_t = (col_sq == source_column(row_sq)).astype(F32).astype(BF)
    a_all = a_ref[...].astype(F32)
    a_flat = jnp.concatenate([a_all[:, 0, :], a_all[:, 1, :]], axis=1).astype(BF)
    aint[...] = dot(a_flat, unmix).astype(BF)
    fas[...] = dot(unmix_t, a_flat, NT).astype(BF).reshape(8, 64, 128)

    pl.semaphore_wait(barrier, 14)

    def b_z(zz):
        return rc(gat.at[core, y, z], gat.at[core, y, z], bz_s.at[zz], bz_r.at[z], zz, c)

    def b_z_in(zz):
        return rc(gat.at[core, y, zz], gat.at[core, y, zz], bz_s.at[zz], bz_r.at[zz], zz, c)

    def b_y(yy, zz):
        return rc(gat.at[core, y, zz], gat.at[core, y, zz], by_s.at[yy, zz], by_r.at[y, zz], z, 2 * yy + core)

    def b_y_in(yy, zz):
        return rc(gat.at[core, yy, zz], gat.at[core, yy, zz], by_s.at[yy, zz], by_r.at[yy, zz], z, 2 * yy + core)

    def b_c(yy):
        return rc(gat.at[core, yy], gat.at[core, yy], bc_s.at[yy], bc_r.at[yy], z, other)

    def b_c_in(yy):
        return rc(gat.at[1 - core, yy], gat.at[1 - core, yy], bc_s.at[yy], bc_r.at[yy], z, other)

    for zz in zpeer:
        b_z(zz).start()
    for yy in ypeer:
        b_y(yy, z).start()

    def f_1(cc):
        return rc(fas.at[cc], fa1.at[c], f1_s.at[cc], f1_r.at[c], z, cc)

    def f_1_in(cc):
        return rc(fas.at[cc], fa1.at[cc], f1_s.at[cc], f1_r.at[cc], z, cc)

    def f_2(zz):
        return rc(fa1.at[zz], fag.at[z], f2_s.at[zz], f2_r.at[z], zz, c)

    def f_2_in(zz):
        return rc(fa1.at[zz], fag.at[zz], f2_s.at[zz], f2_r.at[zz], zz, c)

    def f_3(cc):
        return rc(fag.at[cc], fa3.at[c], f3_s.at[cc], f3_r.at[c], z, cc)

    def f_3_in(cc):
        return rc(fag.at[cc], fa3.at[cc], f3_s.at[cc], f3_r.at[cc], z, cc)

    for cc in cpeer:
        f_1(cc).start()
    fa1[c] = fas[c]

    def b_forward(zz):
        b_z_in(zz).wait_recv()
        for yy in ypeer:
            b_y(yy, zz).start()

    @pl.loop(1, 8)
    def _(t):
        pl.when(z - t >= 0)(lambda: b_forward(z - t))
        pl.when(z + t <= 7)(lambda: b_forward(z + t))

    b_c(y).start()

    for cc in cpeer:
        f_1_in(cc).wait_recv()
    for zz in zpeer:
        f_2(zz).start()
    fag[z] = fa1[z]

    row_i = lax.broadcasted_iota(jnp.int32, (128, 128), 0)
    col_i = lax.broadcasted_iota(jnp.int32, (128, 128), 1)
    pick = (col_i == ((row_i & 63) >> 3) * 16 + (row_i >> 6) * 8 + (row_i & 7)).astype(F32).astype(BF)

    def unpack(cc, yy):
        both = dot(pick, gat[cc, yy].reshape(128, 512)).astype(BF)
        rows = pl.ds(pl.multiple_of((cc * 4 + yy) * 64, 64), 64)
        ball[rows, 0:512] = both[0:64]
        ball[rows, 512:1024] = both[64:128]

    unpack(core, y)
    w_copy.wait()

    @pl.loop(0, 8)
    def _(i):
        rows = pl.ds(pl.multiple_of(i * 16, 16), 16)
        piece = wv[rows].astype(F32)
        wk[0, rows, :] = piece[:, 0, :].astype(BF)
        wk[1, rows, :] = piece[:, 1, :].astype(BF)

    for yy in ypeer:
        for zz in zpeer + [z]:
            b_y_in(yy, zz).wait_recv()
        b_c(yy).start()
        unpack(core, yy)
    for yy in [y] + ypeer:
        b_c_in(yy).wait_recv()
        unpack(1 - core, yy)

    lane_k = (lax.broadcasted_iota(jnp.int32, (128, C2), 1) >> 2) & 1
    sub_k = (lax.broadcasted_iota(jnp.int32, (C2, 128), 0) >> 2) & 1

    proj = None
    for k in range(2):
        a_k = jnp.where(lane_k == k, aint[...].astype(F32), 0.0).astype(BF)
        diff = (wk[k].astype(F32) - dot(a_k, ball[...])).astype(BF)
        part = dot(ball[...], diff, NT)
        proj = part if k == 0 else jnp.where(sub_k == 1, part, proj)
    own = enc(proj)
    xg[z] = own

    def x_out(direction, s, q, zz):
        piece = xg.at[s, pl.ds(q * 128, 128)]
        return rc(piece, piece, xg_s.at[direction, s, q], xg_r.at[s, q], zz, c)

    up, down = lax.rem(z + 1, 8), lax.rem(z + 7, 8)
    for q in range(4):
        pl.when(z < 7)(lambda: x_out(0, z, q, up).start())
        pl.when(z > 0)(lambda: x_out(1, z, q, down).start())

    def x_decode(s, q):
        rows = pl.ds(q * 128, 128)
        lanes = pl.ds(pl.multiple_of(s * 128, 128), 128)
        hi, lo = split(dec(xg[s, rows]))
        xh[rows, lanes] = hi
        xl[rows, lanes] = lo

    def p_add(s, q):
        lanes = pl.ds(pl.multiple_of(s * 128, 128), 128)
        wide = pl.ds(pl.multiple_of(s * 256, 256), 256)
        hi = xh[:, lanes]
        c_hi = chi[q * 256:(q + 1) * 256, lanes]
        c_both = ccat[q * 256:(q + 1) * 256, wide]
        total = dot(jnp.concatenate([hi, hi], axis=1), c_both, NT) + dot(xl[:, lanes], c_hi, NT)
        total = total * (4.0 / O)
        pb[2 * q] = pb[2 * q] + total[:, 0:128]
        pb[2 * q + 1] = pb[2 * q + 1] + total[:, 128:256]

    cov_copy.wait()

    @pl.loop(0, 8)
    def _(i):
        rows = pl.ds(pl.multiple_of(i * 128, 128), 128)
        hi, lo = split(cov[rows, :])
        chi[rows, :] = hi
        clo[rows, :] = lo
        for s in range(8):
            ccat[rows, s * 256:s * 256 + 128] = hi[:, s * 128:(s + 1) * 128]
            ccat[rows, s * 256 + 128:(s + 1) * 256] = lo[:, s * 128:(s + 1) * 128]
        pb[i] = jnp.zeros((C2, 128), F32)

    for q in range(4):
        x_decode(z, q)

    @pl.loop(1, 8)
    def _(t):
        lo_s, hi_s = z - t, z + t
        for q in range(4):
            @pl.when(lo_s >= 0)
            def _():
                x_out(0, lo_s, q, up).wait_recv()
                pl.when(z < 7)(lambda: x_out(0, lo_s, q, up).start())

            @pl.when(hi_s <= 7)
            def _():
                x_out(1, hi_s, q, down).wait_recv()
                pl.when(z > 0)(lambda: x_out(1, hi_s, q, down).start())

            pl.when(lo_s >= 0)(lambda: x_decode(lo_s, q))
            pl.when(hi_s <= 7)(lambda: x_decode(hi_s, q))
            pl.when(lo_s + 1 >= 0)(lambda: p_add(lo_s + 1, q))
            pl.when(jnp.logical_and(t > 1, hi_s - 1 <= 7))(lambda: p_add(hi_s - 1, q))

        @pl.when(t == 2)
        def _():
            for zz in zpeer:
                f_2_in(zz).wait_recv()
            for cc in cpeer:
                f_3(cc).start()
            fa3[c] = fag[c]

    for q in range(4):
        pl.when(z == 7)(lambda: p_add(0, q))
        pl.when(z == 0)(lambda: p_add(7, q))

    def p_c(yy):
        return rc(pes.at[yy], per_.at[yy], pc_s.at[yy], pc_r.at[yy], z, other)

    def p_y(yy):
        return rc(ses.at[yy], ser.at[y], ps_s.at[yy], ps_r.at[y], z, 2 * yy + core)

    def p_y_in(yy):
        return rc(ses.at[yy], ser.at[yy], ps_s.at[yy], ps_r.at[yy], z, 2 * yy + core)

    for yy in ypeer + [y]:
        pes[yy] = enc(pb[2 * yy + 1 - core])
        p_c(yy).start()

    for yy in ypeer:
        p_c(yy).wait_recv()
        ses[yy] = enc(pb[2 * yy + core] + dec(per_[yy]))
        p_y(yy).start()
    p_c(y).wait_recv()
    new_a = pb[c] + dec(per_[y])
    for cc in cpeer:
        f_3_in(cc).wait_recv()
    new_a = new_a + fa3[...].reshape(C2, 128).astype(F32)
    for yy in ypeer:
        p_y_in(yy).wait_recv()
        new_a = new_a + dec(ser[yy])
    nag[c] = enc(new_a).reshape(8, 64, 128)

    def n_y(yy):
        return rc(nag.at[c], nag.at[c], ny_s.at[yy], ng_r.at[c], z, 2 * yy + core)

    def n_c(yy):
        piece = nag.at[2 * yy + core]
        return rc(piece, piece, nc_s.at[yy], ng_r.at[2 * yy + core], z, other)

    def n_in(j):
        return rc(nag.at[j], nag.at[j], nc_s.at[0], ng_r.at[j], z, other)

    for yy in ypeer:
        n_y(yy).start()
    n_c(y).start()

    def n_decode(j):
        lanes = pl.ds(pl.multiple_of(j * 128, 128), 128)
        hi, lo = split(dec(nag[j].reshape(C2, 128)))
        xh[:, lanes] = hi
        xl[:, lanes] = lo

    def t_z(zz):
        return rc(nag.at[zz, c], tz.at[z], tz_s.at[zz], tz_r.at[z], zz, c)

    def t_z_in(zz):
        return rc(nag.at[zz, c], tz.at[zz], tz_s.at[zz], tz_r.at[zz], zz, c)

    def t_n(r):
        return rc(tz.at[r], tn.at[c], tn_s.at[r], tn_r.at[c], z, r)

    def t_n_in(r):
        return rc(tz.at[r], tn.at[r], tn_s.at[r], tn_r.at[r], z, r)

    def n_take(j):
        pl.when(j != z)(lambda: t_z(j).start())
        n_decode(j)

    def f_add(yy, first=False):
        pair = pl.ds(pl.multiple_of(yy * 256, 256), 256)

        @pl.loop(0, 4)
        def _(i):
            lanes = pl.ds(pl.multiple_of(i * 256, 256), 256)
            c_hi = chi[pair, lanes]
            total = dot(xh[:, pair], c_hi) + dot(xl[:, pair], c_hi) + dot(xh[:, pair], clo[pair, lanes])
            total = total * FIELD_DOWN
            if first:
                fb[2 * i] = total[:, 0:128]
                fb[2 * i + 1] = total[:, 128:256]
            else:
                fb[2 * i] = fb[2 * i] + total[:, 0:128]
                fb[2 * i + 1] = fb[2 * i + 1] + total[:, 128:256]

    def n_near(yy):
        n_in(2 * yy + core).wait_recv()
        n_c(yy).start()
        n_take(2 * yy + core)

    def n_far(yy):
        n_in(2 * yy + 1 - core).wait_recv()
        n_take(2 * yy + 1 - core)

    n_take(c)
    n_far(y)
    f_add(y, True)
    n_near(ypeer[0])
    n_near(ypeer[1])
    n_far(ypeer[0])
    f_add(ypeer[0])
    n_near(ypeer[2])
    n_far(ypeer[1])
    f_add(ypeer[1])
    n_far(ypeer[2])
    tz[z] = nag[z, c]
    f_add(ypeer[2])

    def z_out(direction, dest, q, zz):
        rows = pl.ds(q * 128, 128)
        return rc(
            zs.at[direction, dest, rows], zr.at[direction, dest, rows],
            zr_s.at[direction, dest, q], zr_r.at[direction, dest, q], zz, c,
        )

    def z_step(direction, dest, first, last, zz):
        for q in range(4):
            rows = pl.ds(q * 128, 128)

            @pl.when(jnp.logical_and(first, jnp.logical_not(last)))
            def _():
                zs[direction, dest, rows] = enc(fb[dest, rows])

            @pl.when(jnp.logical_not(first))
            def _():
                z_out(direction, dest, q, zz).wait_recv()
                total = fb[dest, rows] + dec(zr[direction, dest, rows])

                @pl.when(last)
                def _():
                    fb[dest, rows] = total

                @pl.when(jnp.logical_not(last))
                def _():
                    zs[direction, dest, rows] = enc(total)

            @pl.when(jnp.logical_not(last))
            def _():
                z_out(direction, dest, q, zz).start()

    @pl.loop(0, 8)
    def _(t):
        @pl.when(t >= z)
        def _():
            z_step(0, 7 + z - t, z == 0, t == 7, up)

        @pl.when(t >= 7 - z)
        def _():
            z_step(1, t - 7 + z, z == 7, t == 7, down)

        @pl.when(t == 3)
        def _():
            for zz in zpeer:
                t_z_in(zz).wait_recv()
            for r in cpeer:
                t_n(r).start()
            tn[c] = tz[c]

        @pl.when(t == 6)
        def _():
            for r in cpeer:
                t_n_in(r).wait_recv()
            rows_a = dec(tn[...].reshape(C2, 128)).T
            hi, lo = split(rows_a)
            lo2 = (rows_a - hi.astype(F32) - lo.astype(F32)).astype(BF)
            back = (lax.broadcasted_iota(jnp.int32, shape_sq, 0) == source_column(lax.broadcasted_iota(jnp.int32, shape_sq, 1))).astype(F32).astype(BF)
            na_ref[...] = dot(hi, back, NT) + dot(lo, back, NT) + dot(lo2, back, NT)
            for k in range(2):
                hi_k = jnp.where(lane_k == k, hi.astype(F32), 0.0).astype(BF)
                lo_k = jnp.where(lane_k == k, lo.astype(F32), 0.0).astype(BF)
                fit = dot(hi_k, ball[...]) + dot(lo_k, ball[...])
                d2[k * 128:(k + 1) * 128, :] = (wk[k].astype(F32) - fit).astype(BF)

    field = fb[z] * (FIELD_UP * 8.0 / D)
    wide = jnp.concatenate([jnp.where(sub_k == 0, field, 0.0), jnp.where(sub_k == 1, field, 0.0)], axis=1)
    hi, lo = split(wide)
    xh[:, 0:256] = hi
    xl[:, 0:256] = lo

    def f_c(h):
        return rc(fcs.at[h], fcr.at[h], fc_s.at[h], fc_r.at[h], z, other)

    def f_y(h, yy):
        return rc(fys.at[h, yy], fyr.at[h, y], fy_s.at[h, yy], fy_r.at[h, y], z, 2 * yy + core)

    def f_y_in(h, yy):
        return rc(fys.at[h, yy], fyr.at[h, yy], fy_s.at[h, yy], fy_r.at[h, yy], z, 2 * yy + core)

    def f_z(h, zz):
        return rc(fzs.at[h, zz], fzr.at[h, z], fz_s.at[h, zz], fz_r.at[h, z], zz, c)

    def f_z_in(h, zz):
        return rc(fzs.at[h, zz], fzr.at[h, zz], fz_s.at[h, zz], fz_r.at[h, zz], zz, c)

    def half(which, h):
        rows = pl.ds(pl.multiple_of(which * 256, 256), 256)
        right = d2[:, h * 512:(h + 1) * 512]
        return (dot(xh[rows, 0:256], right) + dot(xl[rows, 0:256], right)).reshape(4, 64, 512)

    for h in range(2):
        fcs[h] = enc(half(1 - core, h))
        f_c(h).start()
    for h in range(2):
        p2[h] = half(core, h)
        f_c(h).wait_recv()
        for yy in ypeer:
            fys[h, yy] = enc(p2[h, yy] + dec(fcr[h, yy]))
            f_y(h, yy).start()
    for h in range(2):
        total = p2[h, y] + dec(fcr[h, y])
        for yy in ypeer:
            f_y_in(h, yy).wait_recv()
            total = total + dec(fyr[h, yy])
        fsum[h] = total.reshape(8, 8, 512)
        for zz in zpeer:
            mine = fsum[h, zz]
            fzs[h, zz] = enc(jnp.concatenate([mine[:, 0:256], mine[:, 256:512]], axis=0))
            f_z(h, zz).start()
    for h in range(2):
        rest = None
        for zz in zpeer:
            f_z_in(h, zz).wait_recv()
            got = dec(fzr[h, zz])
            rest = got if rest is None else rest + got
        gained = fsum[h, z] + jnp.concatenate([rest[0:8], rest[8:16]], axis=1)
        nb_ref[:, h * 512:(h + 1) * 512] = b_own[:, h * 512:(h + 1) * 512] + gained

    for zz in zpeer:
        b_z(zz).wait_send()
        f_2(zz).wait_send()
        t_z(zz).wait_send()
        for h in range(2):
            f_z(h, zz).wait_send()
        for yy in ypeer:
            b_y(yy, zz).wait_send()
    for r in cpeer:
        t_n(r).wait_send()
        f_1(r).wait_send()
        f_3(r).wait_send()
    for yy in ypeer:
        b_y(yy, z).wait_send()
        p_y(yy).wait_send()
        n_y(yy).wait_send()
        for h in range(2):
            f_y(h, yy).wait_send()
    for yy in ypeer + [y]:
        b_c(yy).wait_send()
        p_c(yy).wait_send()
        n_c(yy).wait_send()
    for h in range(2):
        f_c(h).wait_send()

    @pl.loop(0, 8)
    def _(s):
        for q in range(4):
            pl.when(jnp.logical_and(s <= z, z < 7))(lambda: x_out(0, s, q, up).wait_send())
            pl.when(jnp.logical_and(s >= z, z > 0))(lambda: x_out(1, s, q, down).wait_send())
            pl.when(s > z)(lambda: z_out(0, s, q, up).wait_send())
            pl.when(s < z)(lambda: z_out(1, s, q, down).wait_send())


def per_device(covariance, weight, factor_a, factor_b):
    n = weight.shape[0]
    vm = pl.BlockSpec(memory_space=pltpu.VMEM)
    blk = (8, C2, 128)
    dma = pltpu.SemaphoreType.DMA
    new_a, new_b = pl.pallas_call(
        kernel,
        name="refine",
        out_shape=(jax.ShapeDtypeStruct((n, C2), F32), jax.ShapeDtypeStruct((8, O), F32)),
        in_specs=[pl.BlockSpec(memory_space=pl.ANY), pl.BlockSpec(memory_space=pl.ANY), vm, vm],
        out_specs=(vm, vm),
        scratch_shapes=[
            pltpu.VMEM((1024, 1024), F32),
            pltpu.VMEM((n, 2, O), BF),
            pltpu.VMEM((2, n, O), BF),
            pltpu.VMEM((1024, 1024), BF),
            pltpu.VMEM((1024, 1024), BF),
            pltpu.VMEM((1024, 2048), BF),
            pltpu.VMEM((2, 4, 8, 16, 512), BF),
            pltpu.VMEM((C2, O), BF),
            pltpu.VMEM((128, C2), BF),
            pltpu.VMEM(blk, BF),
            pltpu.VMEM((C2, 1024), BF),
            pltpu.VMEM((C2, 1024), BF),
            pltpu.VMEM((8, 64, 128), BF),
            pltpu.VMEM((8, 64, 128), BF),
            pltpu.VMEM((8, 64, 128), BF),
            pltpu.VMEM((8, 64, 128), BF),
            pltpu.VMEM(blk, F32),
            pltpu.VMEM((4, C2, 128), BF),
            pltpu.VMEM((4, C2, 128), BF),
            pltpu.VMEM((4, C2, 128), BF),
            pltpu.VMEM((4, C2, 128), BF),
            pltpu.VMEM((8, 8, 64, 128), BF),
            pltpu.VMEM((8, 64, 128), BF),
            pltpu.VMEM((8, 64, 128), BF),
            pltpu.VMEM(blk, F32),
            pltpu.VMEM((2,) + blk, BF),
            pltpu.VMEM((2,) + blk, BF),
            pltpu.VMEM((256, O), BF),
            pltpu.VMEM((2, 4, 64, 512), F32),
            pltpu.VMEM((2, 4, 64, 512), BF),
            pltpu.VMEM((2, 4, 64, 512), BF),
            pltpu.VMEM((2, 4, 64, 512), BF),
            pltpu.VMEM((2, 4, 64, 512), BF),
            pltpu.VMEM((2, 8, 8, 512), F32),
            pltpu.VMEM((2, 8, 16, 256), BF),
            pltpu.VMEM((2, 8, 16, 256), BF),
            dma, dma,
            dma((8,)), dma((8,)), dma((4, 8)), dma((4, 8)), dma((4,)), dma((4,)),
            dma((8,)), dma((8,)), dma((8,)), dma((8,)), dma((8,)), dma((8,)),
            dma((2, 8, 4)), dma((8, 4)),
            dma((4,)), dma((4,)), dma((4,)), dma((4,)),
            dma((4,)), dma((4,)), dma((8,)),
            dma((8,)), dma((8,)), dma((8,)), dma((8,)),
            dma((2, 8, 4)), dma((2, 8, 4)),
            dma((2,)), dma((2,)), dma((2, 4)), dma((2, 4)), dma((2, 8)), dma((2, 8)),
        ],
        compiler_params=pltpu.CompilerParams(
            collective_id=0, has_side_effects=True, vmem_limit_bytes=56 * 2**20
        ),
    )(covariance, weight, factor_a, factor_b)
    return new_a.reshape(n, 2, R), new_b.reshape(2, 4, O)


def solution(mesh):
    in_specs = (
        P(("layer", "row"), "col"),
        P(("layer", "col", "row"), None, None),
        P(("layer", "col", "row"), None, None),
        P("layer", ("row", "col"), None),
    )
    out_specs = (P(("layer", "col", "row"), None, None), P("layer", ("row", "col"), None))
    return jax.shard_map(
        per_device, mesh=mesh, in_specs=in_specs, out_specs=out_specs, check_vma=False
    )
```

```python
import functools

import jax
import jax.numpy as jnp
from jax import lax
from jax.experimental import pallas as pl
from jax.experimental.pallas import tpu as pltpu
from jax.sharding import PartitionSpec as P

MESH = pl.DeviceIdType.MESH
F32 = jnp.float32
BF = jnp.bfloat16
D = 8192
O = 1024
R = 256
C2 = 2 * R
FIELD_DOWN = 1.0 / 256.0
FIELD_UP = 256.0

NN = (((1,), (0,)), ((), ()))
NT = (((1,), (1,)), ((), ()))


def enc(x):
    s = x * x
    s = s * s
    return jnp.where(x < 0, -s, s).astype(BF)


def dec(v):
    f = v.astype(F32)
    r = jnp.sqrt(jnp.sqrt(jnp.abs(f)))
    return jnp.where(f < 0, -r, r)


def split(x):
    hi = x.astype(BF)
    return hi, (x - hi.astype(F32)).astype(BF)


def dot(a, b, dims=NN):
    return lax.dot_general(a, b, dims, preferred_element_type=F32)


def source_column(i):
    core = i >> 8
    y = (i >> 6) & 3
    z = (i >> 3) & 7
    k = (i >> 2) & 1
    return k * R + 4 * (z * 8 + y * 2 + core) + (i & 3)


def kernel(
    cov_hbm, w_hbm, a_ref, b_ref, na_ref, nb_ref,
    cov, wv, wk, chi, clo, ccat, gat, ball, aint, xg, xh, xl, fas, fa1, fag, fa3, pb, pes, per_, ses, ser,
    nag, tz, tn, fb, zms, zmr, zs, zr, d2, p2, fcs, fcr, fys, fyr, fsum, fzs, fzr,
    cov_sem, w_sem, bz_s, bz_r, by_s, by_r, bc_s, bc_r, f1_s, f1_r, f2_s, f2_r, f3_s, f3_r, xg_s, xg_r,
    pc_s, pc_r, ps_s, ps_r, ny_s, nc_s, ng_r, tz_s, tz_r, tn_s, tn_r, zm_s, zm_r, zr_s, zr_r,
    fc_s, fc_r, fy_s, fy_r, fz_s, fz_r,
):
    layer = lax.axis_index("layer")
    z = lax.axis_index("row")
    c = lax.axis_index("col")
    y = lax.div(c, 2)
    core = lax.rem(c, 2)
    other = c + 1 - 2 * core
    m = lax.div(z, 2)
    par = lax.rem(z, 2)
    mate = z + 1 - 2 * par
    up, down = lax.rem(z + 2, 8), lax.rem(z + 6, 8)

    def rc(src, dst, ss, rs, zz, cc):
        return pltpu.make_async_remote_copy(
            src_ref=src, dst_ref=dst, send_sem=ss, recv_sem=rs,
            device_id=(layer, zz, cc), device_id_type=MESH,
        )

    cov_copy = pltpu.make_async_copy(cov_hbm, cov, cov_sem)
    w_copy = pltpu.make_async_copy(w_hbm, wv, w_sem)
    cov_copy.start()
    w_copy.start()

    zpeer = [lax.rem(z + d, 8) for d in (1, 7, 2, 6, 3, 5, 4)]
    ypeer = [lax.rem(y + d, 4) for d in (1, 3, 2)]
    cpeer = [lax.rem(c + d, 8) for d in range(1, 8)]

    barrier = pltpu.get_barrier_semaphore()
    for zz in zpeer:
        pl.semaphore_signal(barrier, inc=1, device_id=(layer, zz, c), device_id_type=MESH)
    for cc in cpeer:
        pl.semaphore_signal(barrier, inc=1, device_id=(layer, z, cc), device_id_type=MESH)

    b_own = b_ref[...].astype(F32)
    b_own = jnp.concatenate([b_own[0], b_own[1]], axis=0)
    gat[core, y, z] = jnp.concatenate([b_own[:, 0:512], b_own[:, 512:1024]], axis=0).astype(BF)

    shape_sq = (C2, C2)
    row_sq = lax.broadcasted_iota(jnp.int32, shape_sq, 0)
    col_sq = lax.broadcasted_iota(jnp.int32, shape_sq, 1)
    unmix = (row_sq == source_column(col_sq)).astype(F32).astype(BF)
    unmix_t = (col_sq == source_column(row_sq)).astype(F32).astype(BF)
    a_all = a_ref[...].astype(F32)
    a_flat = jnp.concatenate([a_all[:, 0, :], a_all[:, 1, :]], axis=1).astype(BF)
    aint[...] = dot(a_flat, unmix).astype(BF)
    fas[...] = dot(unmix_t, a_flat, NT).astype(BF).reshape(8, 64, 128)

    pl.semaphore_wait(barrier, 14)

    def b_z(zz):
        return rc(gat.at[core, y, z], gat.at[core, y, z], bz_s.at[zz], bz_r.at[z], zz, c)

    def b_z_in(zz):
        return rc(gat.at[core, y, zz], gat.at[core, y, zz], bz_s.at[zz], bz_r.at[zz], zz, c)

    def b_y(yy, zz):
        return rc(gat.at[core, y, zz], gat.at[core, y, zz], by_s.at[yy, zz], by_r.at[y, zz], z, 2 * yy + core)

    def b_y_in(yy, zz):
        return rc(gat.at[core, yy, zz], gat.at[core, yy, zz], by_s.at[yy, zz], by_r.at[yy, zz], z, 2 * yy + core)

    def b_c(yy):
        return rc(gat.at[core, yy], gat.at[core, yy], bc_s.at[yy], bc_r.at[yy], z, other)

    def b_c_in(yy):
        return rc(gat.at[1 - core, yy], gat.at[1 - core, yy], bc_s.at[yy], bc_r.at[yy], z, other)

    for zz in zpeer:
        b_z(zz).start()
    for yy in ypeer:
        b_y(yy, z).start()

    def f_1(cc):
        return rc(fas.at[cc], fa1.at[c], f1_s.at[cc], f1_r.at[c], z, cc)

    def f_1_in(cc):
        return rc(fas.at[cc], fa1.at[cc], f1_s.at[cc], f1_r.at[cc], z, cc)

    def f_2(zz):
        return rc(fa1.at[zz], fag.at[z], f2_s.at[zz], f2_r.at[z], zz, c)

    def f_2_in(zz):
        return rc(fa1.at[zz], fag.at[zz], f2_s.at[zz], f2_r.at[zz], zz, c)

    def f_3(cc):
        return rc(fag.at[cc], fa3.at[c], f3_s.at[cc], f3_r.at[c], z, cc)

    def f_3_in(cc):
        return rc(fag.at[cc], fa3.at[cc], f3_s.at[cc], f3_r.at[cc], z, cc)

    for cc in cpeer:
        f_1(cc).start()
    fa1[c] = fas[c]

    def b_forward(zz):
        b_z_in(zz).wait_recv()
        for yy in ypeer:
            b_y(yy, zz).start()

    def cov_split(i):
        rows = pl.ds(pl.multiple_of(i * 128, 128), 128)
        hi, lo = split(cov[rows, :])
        chi[rows, :] = hi
        clo[rows, :] = lo
        for s in range(8):
            ccat[rows, s * 256:s * 256 + 128] = hi[:, s * 128:(s + 1) * 128]
            ccat[rows, s * 256 + 128:(s + 1) * 256] = lo[:, s * 128:(s + 1) * 128]
        pb[i] = jnp.zeros((C2, 128), F32)

    cov_copy.wait()
    cov_split(0)

    @pl.loop(1, 8)
    def _(t):
        pl.when(z - t >= 0)(lambda: b_forward(z - t))
        pl.when(z + t <= 7)(lambda: b_forward(z + t))
        cov_split(t)

    b_c(y).start()

    for cc in cpeer:
        f_1_in(cc).wait_recv()
    for zz in zpeer:
        f_2(zz).start()
    fag[z] = fa1[z]

    row_i = lax.broadcasted_iota(jnp.int32, (128, 128), 0)
    col_i = lax.broadcasted_iota(jnp.int32, (128, 128), 1)
    pick = (col_i == ((row_i & 63) >> 3) * 16 + (row_i >> 6) * 8 + (row_i & 7)).astype(F32).astype(BF)

    def unpack(cc, yy):
        both = dot(pick, gat[cc, yy].reshape(128, 512)).astype(BF)
        rows = pl.ds(pl.multiple_of((cc * 4 + yy) * 64, 64), 64)
        ball[rows, 0:512] = both[0:64]
        ball[rows, 512:1024] = both[64:128]

    unpack(core, y)
    w_copy.wait()

    @pl.loop(0, 8)
    def _(i):
        rows = pl.ds(pl.multiple_of(i * 16, 16), 16)
        piece = wv[rows].astype(F32)
        wk[0, rows, :] = piece[:, 0, :].astype(BF)
        wk[1, rows, :] = piece[:, 1, :].astype(BF)

    for yy in ypeer:
        for zz in zpeer + [z]:
            b_y_in(yy, zz).wait_recv()
        b_c(yy).start()
        unpack(core, yy)
    for yy in [y] + ypeer:
        b_c_in(yy).wait_recv()
        unpack(1 - core, yy)

    lane_k = (lax.broadcasted_iota(jnp.int32, (128, C2), 1) >> 2) & 1
    sub_k = (lax.broadcasted_iota(jnp.int32, (C2, 128), 0) >> 2) & 1

    proj = None
    for k in range(2):
        a_k = jnp.where(lane_k == k, aint[...].astype(F32), 0.0).astype(BF)
        diff = (wk[k].astype(F32) - dot(a_k, ball[...])).astype(BF)
        part = dot(ball[...], diff, NT)
        proj = part if k == 0 else jnp.where(sub_k == 1, part, proj)
    own = enc(proj)
    xg[z] = own

    def x_out(direction, s, q, zz):
        piece = xg.at[s, pl.ds(q * 128, 128)]
        return rc(piece, piece, xg_s.at[direction, s, q], xg_r.at[s, q], zz, c)

    def x_pass(s, q, more_up, more_down):
        pl.when(more_up)(lambda: x_out(0, s, q, up).start())
        pl.when(more_down)(lambda: x_out(1, s, q, down).start())
        x_out(2, s, q, mate).start()

    def x_decode(s, h):
        rows = pl.ds(h * 256, 256)
        lanes = pl.ds(pl.multiple_of(s * 128, 128), 128)
        hi, lo = split(dec(xg[s, rows]))
        xh[rows, lanes] = hi
        xl[rows, lanes] = lo

    def p_add(s, h):
        rows = pl.ds(h * 256, 256)
        lanes = pl.ds(pl.multiple_of(s * 128, 128), 128)
        wide = pl.ds(pl.multiple_of(s * 256, 256), 256)

        @pl.loop(0, 4)
        def _(i):
            part = pl.ds(pl.multiple_of(i * 256, 256), 256)
            hi = xh[rows, lanes]
            both = jnp.concatenate([hi, hi], axis=1)
            total = dot(both, ccat[part, wide], NT) + dot(xl[rows, lanes], chi[part, lanes], NT)
            total = total * (4.0 / O)
            pb[2 * i, rows] = pb[2 * i, rows] + total[:, 0:128]
            pb[2 * i + 1, rows] = pb[2 * i + 1, rows] + total[:, 128:256]

    def x_use(s, h):
        x_decode(s, h)
        p_add(s, h)

    def x_mate(u, h):
        def take(s):
            for q in (2 * h, 2 * h + 1):
                x_out(2, s, q, mate).wait_recv()
            x_use(s, h)

        if u == 0:
            take(mate)
        else:
            pl.when(m - u >= 0)(lambda: take(2 * (m - u) + 1 - par))
            pl.when(m + u <= 3)(lambda: take(2 * (m + u) + 1 - par))

    def x_step(u, h):
        pair = (2 * h, 2 * h + 1)
        if u == 0:
            for q in pair:
                x_pass(z, q, m < 3, m > 0)
            x_use(z, h)
            return
        low, high = 2 * (m - u) + par, 2 * (m + u) + par

        def come(s, going_up):
            for q in pair:
                x_out(0, s, q, up).wait_recv()
                x_pass(s, q, jnp.logical_and(going_up, m < 3), jnp.logical_and(jnp.logical_not(going_up), m > 0))

        pl.when(m - u >= 0)(lambda: come(low, True))
        pl.when(m + u <= 3)(lambda: come(high, False))
        pl.when(m - u >= 0)(lambda: x_use(low, h))
        pl.when(m + u <= 3)(lambda: x_use(high, h))
        x_mate(u - 1, h)

    def left_factors():
        for zz in zpeer:
            f_2_in(zz).wait_recv()
        for cc in cpeer:
            f_3(cc).start()
        fa3[c] = fag[c]

    def cols(h):
        return pl.ds(h * 256, 256)

    def p_c(h, yy):
        return rc(pes.at[yy, cols(h)], per_.at[yy, cols(h)], pc_s.at[h, yy], pc_r.at[h, yy], z, other)

    def p_y(h, yy):
        return rc(ses.at[yy, cols(h)], ser.at[y, cols(h)], ps_s.at[h, yy], ps_r.at[h, y], z, 2 * yy + core)

    def p_y_in(h, yy):
        return rc(ses.at[yy, cols(h)], ser.at[yy, cols(h)], ps_s.at[h, yy], ps_r.at[h, yy], z, 2 * yy + core)

    def p_core(h):
        for yy in ypeer + [y]:
            pes[yy, cols(h)] = enc(pb[2 * yy + 1 - core, cols(h)])
            p_c(h, yy).start()

    def p_plane(h):
        for yy in ypeer:
            p_c(h, yy).wait_recv()
            ses[yy, cols(h)] = enc(pb[2 * yy + core, cols(h)] + dec(per_[yy, cols(h)]))
            p_y(h, yy).start()

    def eighths(h):
        return pl.ds(4 * h, 4)

    def n_y(h, yy):
        piece = nag.at[c, eighths(h)]
        return rc(piece, piece, ny_s.at[h, yy], ng_r.at[h, c], z, 2 * yy + core)

    def n_c(h, yy):
        piece = nag.at[2 * yy + core, eighths(h)]
        return rc(piece, piece, nc_s.at[h, yy], ng_r.at[h, 2 * yy + core], z, other)

    def n_in(h, j):
        piece = nag.at[j, eighths(h)]
        return rc(piece, piece, nc_s.at[h, 0], ng_r.at[h, j], z, other)

    def p_end(h):
        p_c(h, y).wait_recv()
        new_a = pb[c, cols(h)] + dec(per_[y, cols(h)])
        for yy in ypeer:
            p_y_in(h, yy).wait_recv()
            new_a = new_a + dec(ser[yy, cols(h)])
        if h == 0:
            for cc in cpeer:
                f_3_in(cc).wait_recv()
        new_a = new_a + fa3[eighths(h)].reshape(256, 128).astype(F32)
        nag[c, eighths(h)] = enc(new_a).reshape(4, 64, 128)
        for yy in ypeer:
            n_y(h, yy).start()
        n_c(h, y).start()

    x_step(0, 0)
    x_step(1, 0)
    x_step(0, 1)
    x_step(2, 0)
    x_step(1, 1)
    x_step(3, 0)
    left_factors()
    x_step(2, 1)
    x_mate(3, 0)
    p_core(0)
    x_step(3, 1)
    p_plane(0)
    x_mate(3, 1)
    p_core(1)
    p_plane(1)
    p_end(0)
    p_end(1)

    def t_z(zz):
        return rc(nag.at[zz, c], tz.at[z], tz_s.at[zz], tz_r.at[z], zz, c)

    def t_z_in(zz):
        return rc(nag.at[zz, c], tz.at[zz], tz_s.at[zz], tz_r.at[zz], zz, c)

    def t_n(r):
        return rc(tz.at[r], tn.at[c], tn_s.at[r], tn_r.at[c], z, r)

    def t_n_in(r):
        return rc(tz.at[r], tn.at[r], tn_s.at[r], tn_r.at[r], z, r)

    def n_take(j, h):
        if h == 1:
            pl.when(j != z)(lambda: t_z(j).start())
        lanes = pl.ds(pl.multiple_of(j * 128, 128), 128)
        hi, lo = split(dec(nag[j, eighths(h)].reshape(256, 128)))
        xh[cols(h), lanes] = hi
        xl[cols(h), lanes] = lo

    def f_add(yy, h, first=False):
        pair = pl.ds(pl.multiple_of(yy * 256, 256), 256)
        rows = cols(h)

        @pl.loop(0, 4)
        def _(i):
            lanes = pl.ds(pl.multiple_of(i * 256, 256), 256)
            c_hi = chi[pair, lanes]
            total = dot(xh[rows, pair], c_hi) + dot(xl[rows, pair], c_hi) + dot(xh[rows, pair], clo[pair, lanes])
            total = total * FIELD_DOWN
            if first:
                fb[2 * i, rows] = total[:, 0:128]
                fb[2 * i + 1, rows] = total[:, 128:256]
            else:
                fb[2 * i, rows] = fb[2 * i, rows] + total[:, 0:128]
                fb[2 * i + 1, rows] = fb[2 * i + 1, rows] + total[:, 128:256]

    def n_near(yy, h):
        n_in(h, 2 * yy + core).wait_recv()
        n_c(h, yy).start()
        n_take(2 * yy + core, h)

    def n_far(yy, h):
        n_in(h, 2 * yy + 1 - core).wait_recv()
        n_take(2 * yy + 1 - core, h)

    def second(h):
        n_take(c, h)
        n_far(y, h)
        f_add(y, h, True)
        n_near(ypeer[0], h)
        n_near(ypeer[1], h)
        n_far(ypeer[0], h)
        f_add(ypeer[0], h)
        n_near(ypeer[2], h)
        n_far(ypeer[1], h)
        f_add(ypeer[1], h)
        n_far(ypeer[2], h)
        f_add(ypeer[2], h)

    def z_mate(d, q):
        rows = pl.ds(q * 128, 128)
        return rc(zms.at[d, rows], zmr.at[d, rows], zm_s.at[d, q], zm_r.at[d, q], mate, c)

    def z_out(direction, d, q, zz):
        rows = pl.ds(q * 128, 128)
        return rc(
            zs.at[direction, d, rows], zr.at[direction, d, rows],
            zr_s.at[direction, d, q], zr_r.at[direction, d, q], zz, c,
        )

    def z_start(h):
        for k in range(4):
            d = 2 * lax.select(m < 2, 3 - k, k) + 1 - par
            for q in (2 * h, 2 * h + 1):
                rows = pl.ds(q * 128, 128)
                zms[d, rows] = enc(fb[d, rows])
                z_mate(d, q).start()

    def z_pass(direction, d, h, first, zz):
        for q in (2 * h, 2 * h + 1):
            rows = pl.ds(q * 128, 128)
            z_mate(d, q).wait_recv()

            @pl.when(first)
            def _():
                zs[direction, d, rows] = enc(fb[d, rows] + dec(zmr[d, rows]))

            @pl.when(jnp.logical_not(first))
            def _():
                z_out(direction, d, q, zz).wait_recv()
                zs[direction, d, rows] = enc(fb[d, rows] + dec(zmr[d, rows]) + dec(zr[direction, d, rows]))

            z_out(direction, d, q, zz).start()

    def z_step(t, h):
        pl.when(t >= m)(lambda: z_pass(0, 2 * (3 + m - t) + par, h, m == 0, up))
        pl.when(t >= 3 - m)(lambda: z_pass(1, 2 * (t - 3 + m) + par, h, m == 3, down))

    def z_end(h):
        for q in (2 * h, 2 * h + 1):
            rows = pl.ds(q * 128, 128)
            z_mate(z, q).wait_recv()
            fb[z, rows] = fb[z, rows] + dec(zmr[z, rows])

            @pl.when(m > 0)
            def _():
                z_out(0, z, q, up).wait_recv()
                fb[z, rows] = fb[z, rows] + dec(zr[0, z, rows])

            @pl.when(m < 3)
            def _():
                z_out(1, z, q, down).wait_recv()
                fb[z, rows] = fb[z, rows] + dec(zr[1, z, rows])

    second(0)
    z_start(0)
    second(1)
    tz[z] = nag[z, c]
    z_start(1)
    z_step(0, 0)
    z_step(1, 0)
    z_step(0, 1)
    z_step(2, 0)
    z_step(1, 1)
    for zz in zpeer:
        t_z_in(zz).wait_recv()
    for r in cpeer:
        t_n(r).start()
    tn[c] = tz[c]
    z_end(0)
    z_step(2, 1)
    for r in cpeer:
        t_n_in(r).wait_recv()
    rows_a = dec(tn[...].reshape(C2, 128)).T
    hi, lo = split(rows_a)
    lo2 = (rows_a - hi.astype(F32) - lo.astype(F32)).astype(BF)
    back = (lax.broadcasted_iota(jnp.int32, shape_sq, 0) == source_column(lax.broadcasted_iota(jnp.int32, shape_sq, 1))).astype(F32).astype(BF)
    na_ref[...] = dot(hi, back, NT) + dot(lo, back, NT) + dot(lo2, back, NT)
    for k in range(2):
        hi_k = jnp.where(lane_k == k, hi.astype(F32), 0.0).astype(BF)
        lo_k = jnp.where(lane_k == k, lo.astype(F32), 0.0).astype(BF)
        fit = dot(hi_k, ball[...]) + dot(lo_k, ball[...])
        d2[k * 128:(k + 1) * 128, :] = (wk[k].astype(F32) - fit).astype(BF)
    z_end(1)

    field = fb[z] * (FIELD_UP * 8.0 / D)
    wide = jnp.concatenate([jnp.where(sub_k == 0, field, 0.0), jnp.where(sub_k == 1, field, 0.0)], axis=1)
    hi, lo = split(wide)
    xh[:, 0:256] = hi
    xl[:, 0:256] = lo

    def f_c(h):
        return rc(fcs.at[h], fcr.at[h], fc_s.at[h], fc_r.at[h], z, other)

    def f_y(h, yy):
        return rc(fys.at[h, yy], fyr.at[h, y], fy_s.at[h, yy], fy_r.at[h, y], z, 2 * yy + core)

    def f_y_in(h, yy):
        return rc(fys.at[h, yy], fyr.at[h, yy], fy_s.at[h, yy], fy_r.at[h, yy], z, 2 * yy + core)

    def f_z(h, zz):
        return rc(fzs.at[h, zz], fzr.at[h, z], fz_s.at[h, zz], fz_r.at[h, z], zz, c)

    def f_z_in(h, zz):
        return rc(fzs.at[h, zz], fzr.at[h, zz], fz_s.at[h, zz], fz_r.at[h, zz], zz, c)

    def half(which, h):
        rows = pl.ds(pl.multiple_of(which * 256, 256), 256)
        right = d2[:, h * 512:(h + 1) * 512]
        return (dot(xh[rows, 0:256], right) + dot(xl[rows, 0:256], right)).reshape(4, 64, 512)

    for h in range(2):
        fcs[h] = enc(half(1 - core, h))
        f_c(h).start()
    for h in range(2):
        p2[h] = half(core, h)
        f_c(h).wait_recv()
        for yy in ypeer:
            fys[h, yy] = enc(p2[h, yy] + dec(fcr[h, yy]))
            f_y(h, yy).start()
    for h in range(2):
        total = p2[h, y] + dec(fcr[h, y])
        for yy in ypeer:
            f_y_in(h, yy).wait_recv()
            total = total + dec(fyr[h, yy])
        fsum[h] = total.reshape(8, 8, 512)
        for zz in zpeer:
            mine = fsum[h, zz]
            fzs[h, zz] = enc(jnp.concatenate([mine[:, 0:256], mine[:, 256:512]], axis=0))
            f_z(h, zz).start()
    for h in range(2):
        rest = None
        for zz in zpeer:
            f_z_in(h, zz).wait_recv()
            got = dec(fzr[h, zz])
            rest = got if rest is None else rest + got
        gained = fsum[h, z] + jnp.concatenate([rest[0:8], rest[8:16]], axis=1)
        nb_ref[:, h * 512:(h + 1) * 512] = b_own[:, h * 512:(h + 1) * 512] + gained

    for zz in zpeer:
        b_z(zz).wait_send()
        f_2(zz).wait_send()
        t_z(zz).wait_send()
        for h in range(2):
            f_z(h, zz).wait_send()
        for yy in ypeer:
            b_y(yy, zz).wait_send()
    for r in cpeer:
        t_n(r).wait_send()
        f_1(r).wait_send()
        f_3(r).wait_send()
    for yy in ypeer:
        b_y(yy, z).wait_send()
        for h in range(2):
            p_y(h, yy).wait_send()
            n_y(h, yy).wait_send()
            f_y(h, yy).wait_send()
    for yy in ypeer + [y]:
        b_c(yy).wait_send()
        for h in range(2):
            p_c(h, yy).wait_send()
            n_c(h, yy).wait_send()
    for h in range(2):
        f_c(h).wait_send()

    @pl.loop(0, 4)
    def _(e):
        s = 2 * e + par
        for q in range(4):
            pl.when(jnp.logical_and(e <= m, m < 3))(lambda: x_out(0, s, q, up).wait_send())
            pl.when(jnp.logical_and(e >= m, m > 0))(lambda: x_out(1, s, q, down).wait_send())
            x_out(2, s, q, mate).wait_send()
            z_mate(2 * e + 1 - par, q).wait_send()
            pl.when(e > m)(lambda: z_out(0, s, q, up).wait_send())
            pl.when(e < m)(lambda: z_out(1, s, q, down).wait_send())


def per_device(covariance, weight, factor_a, factor_b):
    n = weight.shape[0]
    vm = pl.BlockSpec(memory_space=pltpu.VMEM)
    blk = (8, C2, 128)
    dma = pltpu.SemaphoreType.DMA
    new_a, new_b = pl.pallas_call(
        kernel,
        name="refine",
        out_shape=(jax.ShapeDtypeStruct((n, C2), F32), jax.ShapeDtypeStruct((8, O), F32)),
        in_specs=[pl.BlockSpec(memory_space=pl.ANY), pl.BlockSpec(memory_space=pl.ANY), vm, vm],
        out_specs=(vm, vm),
        scratch_shapes=[
            pltpu.VMEM((1024, 1024), F32),
            pltpu.VMEM((n, 2, O), BF),
            pltpu.VMEM((2, n, O), BF),
            pltpu.VMEM((1024, 1024), BF),
            pltpu.VMEM((1024, 1024), BF),
            pltpu.VMEM((1024, 2048), BF),
            pltpu.VMEM((2, 4, 8, 16, 512), BF),
            pltpu.VMEM((C2, O), BF),
            pltpu.VMEM((128, C2), BF),
            pltpu.VMEM(blk, BF),
            pltpu.VMEM((C2, 1024), BF),
            pltpu.VMEM((C2, 1024), BF),
            pltpu.VMEM((8, 64, 128), BF),
            pltpu.VMEM((8, 64, 128), BF),
            pltpu.VMEM((8, 64, 128), BF),
            pltpu.VMEM((8, 64, 128), BF),
            pltpu.VMEM(blk, F32),
            pltpu.VMEM((4, C2, 128), BF),
            pltpu.VMEM((4, C2, 128), BF),
            pltpu.VMEM((4, C2, 128), BF),
            pltpu.VMEM((4, C2, 128), BF),
            pltpu.VMEM((8, 8, 64, 128), BF),
            pltpu.VMEM((8, 64, 128), BF),
            pltpu.VMEM((8, 64, 128), BF),
            pltpu.VMEM(blk, F32),
            pltpu.VMEM(blk, BF),
            pltpu.VMEM(blk, BF),
            pltpu.VMEM((2,) + blk, BF),
            pltpu.VMEM((2,) + blk, BF),
            pltpu.VMEM((256, O), BF),
            pltpu.VMEM((2, 4, 64, 512), F32),
            pltpu.VMEM((2, 4, 64, 512), BF),
            pltpu.VMEM((2, 4, 64, 512), BF),
            pltpu.VMEM((2, 4, 64, 512), BF),
            pltpu.VMEM((2, 4, 64, 512), BF),
            pltpu.VMEM((2, 8, 8, 512), F32),
            pltpu.VMEM((2, 8, 16, 256), BF),
            pltpu.VMEM((2, 8, 16, 256), BF),
            dma, dma,
            dma((8,)), dma((8,)), dma((4, 8)), dma((4, 8)), dma((4,)), dma((4,)),
            dma((8,)), dma((8,)), dma((8,)), dma((8,)), dma((8,)), dma((8,)),
            dma((3, 8, 4)), dma((8, 4)),
            dma((2, 4)), dma((2, 4)), dma((2, 4)), dma((2, 4)),
            dma((2, 4)), dma((2, 4)), dma((2, 8)),
            dma((8,)), dma((8,)), dma((8,)), dma((8,)),
            dma((8, 4)), dma((8, 4)), dma((2, 8, 4)), dma((2, 8, 4)),
            dma((2,)), dma((2,)), dma((2, 4)), dma((2, 4)), dma((2, 8)), dma((2, 8)),
        ],
        compiler_params=pltpu.CompilerParams(
            collective_id=0, has_side_effects=True, vmem_limit_bytes=52 * 2**20
        ),
    )(covariance, weight, factor_a, factor_b)
    return new_a.reshape(n, 2, R), new_b.reshape(2, 4, O)


def solution(mesh):
    in_specs = (
        P(("layer", "row"), "col"),
        P(("layer", "col", "row"), None, None),
        P(("layer", "col", "row"), None, None),
        P("layer", ("row", "col"), None),
    )
    out_specs = (P(("layer", "col", "row"), None, None), P("layer", ("row", "col"), None))
    return jax.shard_map(
        per_device, mesh=mesh, in_specs=in_specs, out_specs=out_specs, check_vma=False
    )
```

```python
import functools

import jax
import jax.numpy as jnp
from jax import lax
from jax.experimental import pallas as pl
from jax.experimental.pallas import tpu as pltpu
from jax.sharding import PartitionSpec as P

MESH = pl.DeviceIdType.MESH
F32 = jnp.float32
BF = jnp.bfloat16
D = 8192
O = 1024
R = 256
C2 = 2 * R
FIELD_DOWN = 1.0 / 256.0
FIELD_UP = 256.0

NN = (((1,), (0,)), ((), ()))
NT = (((1,), (1,)), ((), ()))


def enc(x):
    s = x * x
    s = s * s
    return jnp.where(x < 0, -s, s).astype(BF)


def dec(v):
    f = v.astype(F32)
    r = jnp.sqrt(jnp.sqrt(jnp.abs(f)))
    return jnp.where(f < 0, -r, r)


def split(x):
    hi = x.astype(BF)
    return hi, (x - hi.astype(F32)).astype(BF)


def dot(a, b, dims=NN):
    return lax.dot_general(a, b, dims, preferred_element_type=F32)


def source_column(i):
    core = i >> 8
    y = (i >> 6) & 3
    z = (i >> 3) & 7
    k = (i >> 2) & 1
    return k * R + 4 * (z * 8 + y * 2 + core) + (i & 3)


def kernel(
    cov_hbm, w_hbm, a_ref, b_ref, na_ref, nb_ref,
    cov, wv, wk, chi, clo, ccat, gat, ball, aint, xg, xh, xl, fas, fa1, fag, fa3, pb, pes, per_, ses, ser,
    nag, tz, tn, fb, zs, zr, d2, p2, fcs, fcr, fys, fyr, fsum, fzs, fzr,
    cov_sem, w_sem, bz_s, bz_r, by_s, by_r, bc_s, bc_r, f1_s, f1_r, f2_s, f2_r, f3_s, f3_r, xg_s, xg_r,
    pc_s, pc_r, ps_s, ps_r, ny_s, nc_s, ng_r, tz_s, tz_r, tn_s, tn_r, zr_s, zr_r,
    fc_s, fc_r, fy_s, fy_r, fz_s, fz_r,
):
    layer = lax.axis_index("layer")
    z = lax.axis_index("row")
    c = lax.axis_index("col")
    y = lax.div(c, 2)
    core = lax.rem(c, 2)
    other = c + 1 - 2 * core
    up, down = lax.rem(z + 1, 8), lax.rem(z + 7, 8)

    def rc(src, dst, ss, rs, zz, cc):
        return pltpu.make_async_remote_copy(
            src_ref=src, dst_ref=dst, send_sem=ss, recv_sem=rs,
            device_id=(layer, zz, cc), device_id_type=MESH,
        )

    cov_copy = pltpu.make_async_copy(cov_hbm, cov, cov_sem)
    w_copy = pltpu.make_async_copy(w_hbm, wv, w_sem)
    cov_copy.start()
    w_copy.start()

    zpeer = [lax.rem(z + d, 8) for d in (1, 7, 2, 6, 3, 5, 4)]
    ypeer = [lax.rem(y + d, 4) for d in (1, 3, 2)]
    cpeer = [lax.rem(c + d, 8) for d in range(1, 8)]

    barrier = pltpu.get_barrier_semaphore()
    for zz in zpeer:
        pl.semaphore_signal(barrier, inc=1, device_id=(layer, zz, c), device_id_type=MESH)
    for cc in cpeer:
        pl.semaphore_signal(barrier, inc=1, device_id=(layer, z, cc), device_id_type=MESH)

    b_own = b_ref[...].astype(F32)
    b_own = jnp.concatenate([b_own[0], b_own[1]], axis=0)
    gat[core, y, z] = jnp.concatenate([b_own[:, 0:512], b_own[:, 512:1024]], axis=0).astype(BF)

    shape_sq = (C2, C2)
    row_sq = lax.broadcasted_iota(jnp.int32, shape_sq, 0)
    col_sq = lax.broadcasted_iota(jnp.int32, shape_sq, 1)
    unmix = (row_sq == source_column(col_sq)).astype(F32).astype(BF)
    unmix_t = (col_sq == source_column(row_sq)).astype(F32).astype(BF)
    a_all = a_ref[...].astype(F32)
    a_flat = jnp.concatenate([a_all[:, 0, :], a_all[:, 1, :]], axis=1).astype(BF)
    aint[...] = dot(a_flat, unmix).astype(BF)
    fas[...] = dot(unmix_t, a_flat, NT).astype(BF).reshape(8, 64, 128)

    pl.semaphore_wait(barrier, 14)

    def b_z(zz):
        return rc(gat.at[core, y, z], gat.at[core, y, z], bz_s.at[zz], bz_r.at[z], zz, c)

    def b_z_in(zz):
        return rc(gat.at[core, y, zz], gat.at[core, y, zz], bz_s.at[zz], bz_r.at[zz], zz, c)

    def b_y(yy, zz):
        return rc(gat.at[core, y, zz], gat.at[core, y, zz], by_s.at[yy, zz], by_r.at[y, zz], z, 2 * yy + core)

    def b_y_in(yy, zz):
        return rc(gat.at[core, yy, zz], gat.at[core, yy, zz], by_s.at[yy, zz], by_r.at[yy, zz], z, 2 * yy + core)

    def b_c(yy):
        return rc(gat.at[core, yy], gat.at[core, yy], bc_s.at[yy], bc_r.at[yy], z, other)

    def b_c_in(yy):
        return rc(gat.at[1 - core, yy], gat.at[1 - core, yy], bc_s.at[yy], bc_r.at[yy], z, other)

    for zz in zpeer:
        b_z(zz).start()
    for yy in ypeer:
        b_y(yy, z).start()

    def f_1(cc):
        return rc(fas.at[cc], fa1.at[c], f1_s.at[cc], f1_r.at[c], z, cc)

    def f_1_in(cc):
        return rc(fas.at[cc], fa1.at[cc], f1_s.at[cc], f1_r.at[cc], z, cc)

    def f_2(zz):
        return rc(fa1.at[zz], fag.at[z], f2_s.at[zz], f2_r.at[z], zz, c)

    def f_2_in(zz):
        return rc(fa1.at[zz], fag.at[zz], f2_s.at[zz], f2_r.at[zz], zz, c)

    def f_3(cc):
        return rc(fag.at[cc], fa3.at[c], f3_s.at[cc], f3_r.at[c], z, cc)

    def f_3_in(cc):
        return rc(fag.at[cc], fa3.at[cc], f3_s.at[cc], f3_r.at[cc], z, cc)

    for cc in cpeer:
        f_1(cc).start()
    fa1[c] = fas[c]

    def b_forward(zz):
        b_z_in(zz).wait_recv()
        for yy in ypeer:
            b_y(yy, zz).start()

    def cov_split(i):
        rows = pl.ds(pl.multiple_of(i * 128, 128), 128)
        hi, lo = split(cov[rows, :])
        chi[rows, :] = hi
        clo[rows, :] = lo
        for s in range(8):
            ccat[rows, s * 256:s * 256 + 128] = hi[:, s * 128:(s + 1) * 128]
            ccat[rows, s * 256 + 128:(s + 1) * 256] = lo[:, s * 128:(s + 1) * 128]
        pb[i] = jnp.zeros((C2, 128), F32)

    cov_copy.wait()
    cov_split(0)

    @pl.loop(1, 8)
    def _(t):
        pl.when(z - t >= 0)(lambda: b_forward(z - t))
        pl.when(z + t <= 7)(lambda: b_forward(z + t))
        cov_split(t)

    b_c(y).start()

    for cc in cpeer:
        f_1_in(cc).wait_recv()
    for zz in zpeer:
        f_2(zz).start()
    fag[z] = fa1[z]

    row_i = lax.broadcasted_iota(jnp.int32, (128, 128), 0)
    col_i = lax.broadcasted_iota(jnp.int32, (128, 128), 1)
    pick = (col_i == ((row_i & 63) >> 3) * 16 + (row_i >> 6) * 8 + (row_i & 7)).astype(F32).astype(BF)

    def unpack(cc, yy):
        both = dot(pick, gat[cc, yy].reshape(128, 512)).astype(BF)
        rows = pl.ds(pl.multiple_of((cc * 4 + yy) * 64, 64), 64)
        ball[rows, 0:512] = both[0:64]
        ball[rows, 512:1024] = both[64:128]

    unpack(core, y)
    w_copy.wait()

    @pl.loop(0, 8)
    def _(i):
        rows = pl.ds(pl.multiple_of(i * 16, 16), 16)
        piece = wv[rows].astype(F32)
        wk[0, rows, :] = piece[:, 0, :].astype(BF)
        wk[1, rows, :] = piece[:, 1, :].astype(BF)

    for yy in ypeer:
        for zz in zpeer + [z]:
            b_y_in(yy, zz).wait_recv()
        b_c(yy).start()
        unpack(core, yy)
    for yy in [y] + ypeer:
        b_c_in(yy).wait_recv()
        unpack(1 - core, yy)

    lane_k = (lax.broadcasted_iota(jnp.int32, (128, C2), 1) >> 2) & 1
    sub_k = (lax.broadcasted_iota(jnp.int32, (C2, 128), 0) >> 2) & 1

    proj = None
    for k in range(2):
        a_k = jnp.where(lane_k == k, aint[...].astype(F32), 0.0).astype(BF)
        diff = (wk[k].astype(F32) - dot(a_k, ball[...])).astype(BF)
        part = dot(ball[...], diff, NT)
        proj = part if k == 0 else jnp.where(sub_k == 1, part, proj)
    own = enc(proj)
    xg[z] = own

    def x_out(direction, s, q, zz):
        piece = xg.at[s, pl.ds(q * 128, 128)]
        return rc(piece, piece, xg_s.at[direction, s, q], xg_r.at[s, q], zz, c)

    for q in range(4):
        pl.when(z < 7)(lambda: x_out(0, z, q, up).start())
        pl.when(z > 0)(lambda: x_out(1, z, q, down).start())

    def x_decode(s, q):
        rows = pl.ds(q * 128, 128)
        lanes = pl.ds(pl.multiple_of(s * 128, 128), 128)
        hi, lo = split(dec(xg[s, rows]))
        xh[rows, lanes] = hi
        xl[rows, lanes] = lo

    def p_add(s, q):
        lanes = pl.ds(pl.multiple_of(s * 128, 128), 128)
        wide = pl.ds(pl.multiple_of(s * 256, 256), 256)
        hi = xh[:, lanes]
        c_hi = chi[q * 256:(q + 1) * 256, lanes]
        c_both = ccat[q * 256:(q + 1) * 256, wide]
        total = dot(jnp.concatenate([hi, hi], axis=1), c_both, NT) + dot(xl[:, lanes], c_hi, NT)
        total = total * (4.0 / O)
        pb[2 * q] = pb[2 * q] + total[:, 0:128]
        pb[2 * q + 1] = pb[2 * q + 1] + total[:, 128:256]

    for q in range(4):
        x_decode(z, q)

    @pl.loop(1, 8)
    def _(t):
        lo_s, hi_s = z - t, z + t
        for q in range(4):
            @pl.when(lo_s >= 0)
            def _():
                x_out(0, lo_s, q, up).wait_recv()
                pl.when(z < 7)(lambda: x_out(0, lo_s, q, up).start())

            @pl.when(hi_s <= 7)
            def _():
                x_out(1, hi_s, q, down).wait_recv()
                pl.when(z > 0)(lambda: x_out(1, hi_s, q, down).start())

            pl.when(lo_s >= 0)(lambda: x_decode(lo_s, q))
            pl.when(hi_s <= 7)(lambda: x_decode(hi_s, q))
            pl.when(lo_s + 1 >= 0)(lambda: p_add(lo_s + 1, q))
            pl.when(jnp.logical_and(t > 1, hi_s - 1 <= 7))(lambda: p_add(hi_s - 1, q))

        @pl.when(t == 2)
        def _():
            for zz in zpeer:
                f_2_in(zz).wait_recv()
            for cc in cpeer:
                f_3(cc).start()
            fa3[c] = fag[c]

    for q in range(4):
        pl.when(z == 7)(lambda: p_add(0, q))
        pl.when(z == 0)(lambda: p_add(7, q))

    def cols(h):
        return pl.ds(h * 256, 256)

    def p_c(h, yy):
        return rc(pes.at[yy, cols(h)], per_.at[yy, cols(h)], pc_s.at[h, yy], pc_r.at[h, yy], z, other)

    def p_y(h, yy):
        return rc(ses.at[yy, cols(h)], ser.at[y, cols(h)], ps_s.at[h, yy], ps_r.at[h, y], z, 2 * yy + core)

    def p_y_in(h, yy):
        return rc(ses.at[yy, cols(h)], ser.at[yy, cols(h)], ps_s.at[h, yy], ps_r.at[h, yy], z, 2 * yy + core)

    def p_core(h):
        for yy in ypeer + [y]:
            pes[yy, cols(h)] = enc(pb[2 * yy + 1 - core, cols(h)])
            p_c(h, yy).start()

    def p_plane(h):
        for yy in ypeer:
            p_c(h, yy).wait_recv()
            ses[yy, cols(h)] = enc(pb[2 * yy + core, cols(h)] + dec(per_[yy, cols(h)]))
            p_y(h, yy).start()

    def eighths(h):
        return pl.ds(4 * h, 4)

    def n_y(h, yy):
        piece = nag.at[c, eighths(h)]
        return rc(piece, piece, ny_s.at[h, yy], ng_r.at[h, c], z, 2 * yy + core)

    def n_c(h, yy):
        piece = nag.at[2 * yy + core, eighths(h)]
        return rc(piece, piece, nc_s.at[h, yy], ng_r.at[h, 2 * yy + core], z, other)

    def n_in(h, j):
        piece = nag.at[j, eighths(h)]
        return rc(piece, piece, nc_s.at[h, 0], ng_r.at[h, j], z, other)

    def p_end(h):
        p_c(h, y).wait_recv()
        new_a = pb[c, cols(h)] + dec(per_[y, cols(h)])
        for yy in ypeer:
            p_y_in(h, yy).wait_recv()
            new_a = new_a + dec(ser[yy, cols(h)])
        if h == 0:
            for cc in cpeer:
                f_3_in(cc).wait_recv()
        new_a = new_a + fa3[eighths(h)].reshape(256, 128).astype(F32)
        nag[c, eighths(h)] = enc(new_a).reshape(4, 64, 128)
        for yy in ypeer:
            n_y(h, yy).start()
        n_c(h, y).start()

    p_core(0)
    p_core(1)
    p_plane(0)
    p_plane(1)
    p_end(0)
    p_end(1)

    def t_z(zz):
        return rc(nag.at[zz, c], tz.at[z], tz_s.at[zz], tz_r.at[z], zz, c)

    def t_z_in(zz):
        return rc(nag.at[zz, c], tz.at[zz], tz_s.at[zz], tz_r.at[zz], zz, c)

    def t_n(r):
        return rc(tz.at[r], tn.at[c], tn_s.at[r], tn_r.at[c], z, r)

    def t_n_in(r):
        return rc(tz.at[r], tn.at[r], tn_s.at[r], tn_r.at[r], z, r)

    def n_take(j, h):
        if h == 1:
            pl.when(j != z)(lambda: t_z(j).start())
        lanes = pl.ds(pl.multiple_of(j * 128, 128), 128)
        hi, lo = split(dec(nag[j, eighths(h)].reshape(256, 128)))
        xh[cols(h), lanes] = hi
        xl[cols(h), lanes] = lo

    def f_add(yy, h, first=False):
        pair = pl.ds(pl.multiple_of(yy * 256, 256), 256)
        rows = cols(h)

        @pl.loop(0, 4)
        def _(i):
            lanes = pl.ds(pl.multiple_of(i * 256, 256), 256)
            c_hi = chi[pair, lanes]
            total = dot(xh[rows, pair], c_hi) + dot(xl[rows, pair], c_hi) + dot(xh[rows, pair], clo[pair, lanes])
            total = total * FIELD_DOWN
            if first:
                fb[2 * i, rows] = total[:, 0:128]
                fb[2 * i + 1, rows] = total[:, 128:256]
            else:
                fb[2 * i, rows] = fb[2 * i, rows] + total[:, 0:128]
                fb[2 * i + 1, rows] = fb[2 * i + 1, rows] + total[:, 128:256]

    def n_near(yy, h):
        n_in(h, 2 * yy + core).wait_recv()
        n_c(h, yy).start()
        n_take(2 * yy + core, h)

    def n_far(yy, h):
        n_in(h, 2 * yy + 1 - core).wait_recv()
        n_take(2 * yy + 1 - core, h)

    def second(h):
        n_take(c, h)
        n_far(y, h)
        f_add(y, h, True)
        n_near(ypeer[0], h)
        n_near(ypeer[1], h)
        n_far(ypeer[0], h)
        f_add(ypeer[0], h)
        n_near(ypeer[2], h)
        n_far(ypeer[1], h)
        f_add(ypeer[1], h)
        n_far(ypeer[2], h)
        f_add(ypeer[2], h)

    def z_out(direction, d, q, zz):
        rows = pl.ds(q * 128, 128)
        return rc(
            zs.at[direction, d, rows], zr.at[direction, d, rows],
            zr_s.at[direction, d, q], zr_r.at[direction, d, q], zz, c,
        )

    def z_move(direction, d, q, first, last, zz):
        rows = pl.ds(q * 128, 128)

        @pl.when(jnp.logical_and(first, jnp.logical_not(last)))
        def _():
            zs[direction, d, rows] = enc(fb[d, rows])

        @pl.when(jnp.logical_not(first))
        def _():
            z_out(direction, d, q, zz).wait_recv()
            total = fb[d, rows] + dec(zr[direction, d, rows])

            @pl.when(last)
            def _():
                fb[d, rows] = total

            @pl.when(jnp.logical_not(last))
            def _():
                zs[direction, d, rows] = enc(total)

        @pl.when(jnp.logical_not(last))
        def _():
            z_out(direction, d, q, zz).start()

    def z_step(t, h):
        for q in (2 * h, 2 * h + 1):
            pl.when(t >= z)(lambda: z_move(0, 7 + z - t, q, z == 0, t == 7, up))
            pl.when(t >= 7 - z)(lambda: z_move(1, t - 7 + z, q, z == 7, t == 7, down))

    def natural():
        rows_a = dec(tn[...].reshape(C2, 128)).T
        hi, lo = split(rows_a)
        return rows_a, hi, lo

    def second_difference(k):
        _, hi, lo = natural()
        hi_k = jnp.where(lane_k == k, hi.astype(F32), 0.0).astype(BF)
        lo_k = jnp.where(lane_k == k, lo.astype(F32), 0.0).astype(BF)
        fit = dot(hi_k, ball[...]) + dot(lo_k, ball[...])
        d2[k * 128:(k + 1) * 128, :] = (wk[k].astype(F32) - fit).astype(BF)

    second(0)
    z_step(0, 0)
    second(1)
    tz[z] = nag[z, c]

    @pl.loop(0, 7)
    def _(t):
        z_step(t + 1, 0)
        z_step(t, 1)

        @pl.when(t == 3)
        def _():
            for zz in zpeer:
                t_z_in(zz).wait_recv()
            for r in cpeer:
                t_n(r).start()
            tn[c] = tz[c]

        @pl.when(t == 5)
        def _():
            for r in cpeer:
                t_n_in(r).wait_recv()
            second_difference(0)

        @pl.when(t == 6)
        def _():
            second_difference(1)

    z_step(7, 1)

    field = fb[z] * (FIELD_UP * 8.0 / D)
    wide = jnp.concatenate([jnp.where(sub_k == 0, field, 0.0), jnp.where(sub_k == 1, field, 0.0)], axis=1)
    hi, lo = split(wide)
    xh[:, 0:256] = hi
    xl[:, 0:256] = lo

    def f_c(h):
        return rc(fcs.at[h], fcr.at[h], fc_s.at[h], fc_r.at[h], z, other)

    def f_y(h, yy):
        return rc(fys.at[h, yy], fyr.at[h, y], fy_s.at[h, yy], fy_r.at[h, y], z, 2 * yy + core)

    def f_y_in(h, yy):
        return rc(fys.at[h, yy], fyr.at[h, yy], fy_s.at[h, yy], fy_r.at[h, yy], z, 2 * yy + core)

    def f_z(h, zz):
        return rc(fzs.at[h, zz], fzr.at[h, z], fz_s.at[h, zz], fz_r.at[h, z], zz, c)

    def f_z_in(h, zz):
        return rc(fzs.at[h, zz], fzr.at[h, zz], fz_s.at[h, zz], fz_r.at[h, zz], zz, c)

    def half(which, h):
        rows = pl.ds(pl.multiple_of(which * 256, 256), 256)
        right = d2[:, h * 512:(h + 1) * 512]
        return (dot(xh[rows, 0:256], right) + dot(xl[rows, 0:256], right)).reshape(4, 64, 512)

    for h in range(2):
        fcs[h] = enc(half(1 - core, h))
        f_c(h).start()
    for h in range(2):
        p2[h] = half(core, h)
        f_c(h).wait_recv()
        for yy in ypeer:
            fys[h, yy] = enc(p2[h, yy] + dec(fcr[h, yy]))
            f_y(h, yy).start()
    rows_a, hi, lo = natural()
    lo2 = (rows_a - hi.astype(F32) - lo.astype(F32)).astype(BF)
    back = (lax.broadcasted_iota(jnp.int32, shape_sq, 0) == source_column(lax.broadcasted_iota(jnp.int32, shape_sq, 1))).astype(F32).astype(BF)
    na_ref[...] = dot(hi, back, NT) + dot(lo, back, NT) + dot(lo2, back, NT)
    for h in range(2):
        total = p2[h, y] + dec(fcr[h, y])
        for yy in ypeer:
            f_y_in(h, yy).wait_recv()
            total = total + dec(fyr[h, yy])
        fsum[h] = total.reshape(8, 8, 512)
        for zz in zpeer:
            mine = fsum[h, zz]
            fzs[h, zz] = enc(jnp.concatenate([mine[:, 0:256], mine[:, 256:512]], axis=0))
            f_z(h, zz).start()
    for h in range(2):
        rest = None
        for zz in zpeer:
            f_z_in(h, zz).wait_recv()
            got = dec(fzr[h, zz])
            rest = got if rest is None else rest + got
        gained = fsum[h, z] + jnp.concatenate([rest[0:8], rest[8:16]], axis=1)
        nb_ref[:, h * 512:(h + 1) * 512] = b_own[:, h * 512:(h + 1) * 512] + gained

    for zz in zpeer:
        b_z(zz).wait_send()
        f_2(zz).wait_send()
        t_z(zz).wait_send()
        for h in range(2):
            f_z(h, zz).wait_send()
        for yy in ypeer:
            b_y(yy, zz).wait_send()
    for r in cpeer:
        t_n(r).wait_send()
        f_1(r).wait_send()
        f_3(r).wait_send()
    for yy in ypeer:
        b_y(yy, z).wait_send()
        for h in range(2):
            p_y(h, yy).wait_send()
            n_y(h, yy).wait_send()
            f_y(h, yy).wait_send()
    for yy in ypeer + [y]:
        b_c(yy).wait_send()
        for h in range(2):
            p_c(h, yy).wait_send()
            n_c(h, yy).wait_send()
    for h in range(2):
        f_c(h).wait_send()

    @pl.loop(0, 8)
    def _(s):
        for q in range(4):
            pl.when(jnp.logical_and(s <= z, z < 7))(lambda: x_out(0, s, q, up).wait_send())
            pl.when(jnp.logical_and(s >= z, z > 0))(lambda: x_out(1, s, q, down).wait_send())
            pl.when(s > z)(lambda: z_out(0, s, q, up).wait_send())
            pl.when(s < z)(lambda: z_out(1, s, q, down).wait_send())


def per_device(covariance, weight, factor_a, factor_b):
    n = weight.shape[0]
    vm = pl.BlockSpec(memory_space=pltpu.VMEM)
    blk = (8, C2, 128)
    dma = pltpu.SemaphoreType.DMA
    new_a, new_b = pl.pallas_call(
        kernel,
        name="refine",
        out_shape=(jax.ShapeDtypeStruct((n, C2), F32), jax.ShapeDtypeStruct((8, O), F32)),
        in_specs=[pl.BlockSpec(memory_space=pl.ANY), pl.BlockSpec(memory_space=pl.ANY), vm, vm],
        out_specs=(vm, vm),
        scratch_shapes=[
            pltpu.VMEM((1024, 1024), F32),
            pltpu.VMEM((n, 2, O), BF),
            pltpu.VMEM((2, n, O), BF),
            pltpu.VMEM((1024, 1024), BF),
            pltpu.VMEM((1024, 1024), BF),
            pltpu.VMEM((1024, 2048), BF),
            pltpu.VMEM((2, 4, 8, 16, 512), BF),
            pltpu.VMEM((C2, O), BF),
            pltpu.VMEM((128, C2), BF),
            pltpu.VMEM(blk, BF),
            pltpu.VMEM((C2, 1024), BF),
            pltpu.VMEM((C2, 1024), BF),
            pltpu.VMEM((8, 64, 128), BF),
            pltpu.VMEM((8, 64, 128), BF),
            pltpu.VMEM((8, 64, 128), BF),
            pltpu.VMEM((8, 64, 128), BF),
            pltpu.VMEM(blk, F32),
            pltpu.VMEM((4, C2, 128), BF),
            pltpu.VMEM((4, C2, 128), BF),
            pltpu.VMEM((4, C2, 128), BF),
            pltpu.VMEM((4, C2, 128), BF),
            pltpu.VMEM((8, 8, 64, 128), BF),
            pltpu.VMEM((8, 64, 128), BF),
            pltpu.VMEM((8, 64, 128), BF),
            pltpu.VMEM(blk, F32),
            pltpu.VMEM((2,) + blk, BF),
            pltpu.VMEM((2,) + blk, BF),
            pltpu.VMEM((256, O), BF),
            pltpu.VMEM((2, 4, 64, 512), F32),
            pltpu.VMEM((2, 4, 64, 512), BF),
            pltpu.VMEM((2, 4, 64, 512), BF),
            pltpu.VMEM((2, 4, 64, 512), BF),
            pltpu.VMEM((2, 4, 64, 512), BF),
            pltpu.VMEM((2, 8, 8, 512), F32),
            pltpu.VMEM((2, 8, 16, 256), BF),
            pltpu.VMEM((2, 8, 16, 256), BF),
            dma, dma,
            dma((8,)), dma((8,)), dma((4, 8)), dma((4, 8)), dma((4,)), dma((4,)),
            dma((8,)), dma((8,)), dma((8,)), dma((8,)), dma((8,)), dma((8,)),
            dma((2, 8, 4)), dma((8, 4)),
            dma((2, 4)), dma((2, 4)), dma((2, 4)), dma((2, 4)),
            dma((2, 4)), dma((2, 4)), dma((2, 8)),
            dma((8,)), dma((8,)), dma((8,)), dma((8,)),
            dma((2, 8, 4)), dma((2, 8, 4)),
            dma((2,)), dma((2,)), dma((2, 4)), dma((2, 4)), dma((2, 8)), dma((2, 8)),
        ],
        compiler_params=pltpu.CompilerParams(
            collective_id=0, has_side_effects=True, vmem_limit_bytes=56 * 2**20
        ),
    )(covariance, weight, factor_a, factor_b)
    return new_a.reshape(n, 2, R), new_b.reshape(2, 4, O)


def solution(mesh):
    in_specs = (
        P(("layer", "row"), "col"),
        P(("layer", "col", "row"), None, None),
        P(("layer", "col", "row"), None, None),
        P("layer", ("row", "col"), None),
    )
    out_specs = (P(("layer", "col", "row"), None, None), P("layer", ("row", "col"), None))
    return jax.shard_map(
        per_device, mesh=mesh, in_specs=in_specs, out_specs=out_specs, check_vma=False
    )
```

```python
import functools

import jax
import jax.numpy as jnp
from jax import lax
from jax.experimental import pallas as pl
from jax.experimental.pallas import tpu as pltpu
from jax.sharding import PartitionSpec as P

MESH = pl.DeviceIdType.MESH
F32 = jnp.float32
BF = jnp.bfloat16
D = 8192
O = 1024
R = 256
C2 = 2 * R
FIELD_DOWN = 1.0 / 256.0
FIELD_UP = 256.0

NN = (((1,), (0,)), ((), ()))
NT = (((1,), (1,)), ((), ()))


def enc(x):
    s = x * x
    s = s * s
    return jnp.where(x < 0, -s, s).astype(BF)


def dec(v):
    f = v.astype(F32)
    r = jnp.sqrt(jnp.sqrt(jnp.abs(f)))
    return jnp.where(f < 0, -r, r)


def split(x):
    hi = x.astype(BF)
    return hi, (x - hi.astype(F32)).astype(BF)


def dot(a, b, dims=NN):
    return lax.dot_general(a, b, dims, preferred_element_type=F32)


def source_column(i):
    core = i >> 8
    y = (i >> 6) & 3
    z = (i >> 3) & 7
    k = (i >> 2) & 1
    return k * R + 4 * (z * 8 + y * 2 + core) + (i & 3)


def kernel(
    cov_hbm, w_hbm, a_hbm, b_ref, na_ref, nb_ref,
    cov, wv, av, wk, chi, clo, ccat, gat, ball, aint, xg, xh, xl, fas, fa1, fag, fa3, pb, pes, per_, ses, ser,
    nag, tz, tn, fb, zs, zr, d2, p2, fcs, fcr, fys, fyr, fsum, fzs, fzr,
    cov_sem, w_sem, a_sem, bz_s, bz_r, by_s, by_r, bc_s, bc_r, f1_s, f1_r, f2_s, f2_r, f3_s, f3_r, xg_s, xg_r,
    pc_s, pc_r, ps_s, ps_r, ny_s, nc_s, ng_r, tz_s, tz_r, tn_s, tn_r, zr_s, zr_r,
    fc_s, fc_r, fy_s, fy_r, fz_s, fz_r,
):
    layer = lax.axis_index("layer")
    z = lax.axis_index("row")
    c = lax.axis_index("col")
    y = lax.div(c, 2)
    core = lax.rem(c, 2)
    other = c + 1 - 2 * core
    up, down = lax.rem(z + 1, 8), lax.rem(z + 7, 8)

    def rc(src, dst, ss, rs, zz, cc):
        return pltpu.make_async_remote_copy(
            src_ref=src, dst_ref=dst, send_sem=ss, recv_sem=rs,
            device_id=(layer, zz, cc), device_id_type=MESH,
        )

    cov_copy = pltpu.make_async_copy(cov_hbm, cov, cov_sem)
    w_copy = pltpu.make_async_copy(w_hbm, wv, w_sem)
    a_copy = pltpu.make_async_copy(a_hbm, av, a_sem)
    a_copy.start()
    cov_copy.start()
    w_copy.start()

    zpeer = [lax.rem(z + d, 8) for d in (1, 7, 2, 6, 3, 5, 4)]
    ypeer = [lax.rem(y + d, 4) for d in (1, 3, 2)]
    cpeer = [lax.rem(c + d, 8) for d in range(1, 8)]

    barrier = pltpu.get_barrier_semaphore()
    for zz in zpeer:
        pl.semaphore_signal(barrier, inc=1, device_id=(layer, zz, c), device_id_type=MESH)
    for cc in cpeer:
        pl.semaphore_signal(barrier, inc=1, device_id=(layer, z, cc), device_id_type=MESH)

    b_own = b_ref[...].astype(F32)
    b_own = jnp.concatenate([b_own[0], b_own[1]], axis=0)
    gat[core, y, z] = jnp.concatenate([b_own[:, 0:512], b_own[:, 512:1024]], axis=0).astype(BF)

    pl.semaphore_wait(barrier, 14)

    def b_z(zz):
        return rc(gat.at[core, y, z], gat.at[core, y, z], bz_s.at[zz], bz_r.at[z], zz, c)

    def b_z_in(zz):
        return rc(gat.at[core, y, zz], gat.at[core, y, zz], bz_s.at[zz], bz_r.at[zz], zz, c)

    def b_y(yy, zz):
        return rc(gat.at[core, y, zz], gat.at[core, y, zz], by_s.at[yy, zz], by_r.at[y, zz], z, 2 * yy + core)

    def b_y_in(yy, zz):
        return rc(gat.at[core, yy, zz], gat.at[core, yy, zz], by_s.at[yy, zz], by_r.at[yy, zz], z, 2 * yy + core)

    def b_c(yy):
        return rc(gat.at[core, yy], gat.at[core, yy], bc_s.at[yy], bc_r.at[yy], z, other)

    def b_c_in(yy):
        return rc(gat.at[1 - core, yy], gat.at[1 - core, yy], bc_s.at[yy], bc_r.at[yy], z, other)

    for zz in zpeer:
        b_z(zz).start()
    for yy in ypeer:
        b_y(yy, z).start()

    def f_1(cc):
        return rc(fas.at[cc], fa1.at[c], f1_s.at[cc], f1_r.at[c], z, cc)

    def f_1_in(cc):
        return rc(fas.at[cc], fa1.at[cc], f1_s.at[cc], f1_r.at[cc], z, cc)

    def f_2(zz):
        return rc(fa1.at[zz], fag.at[z], f2_s.at[zz], f2_r.at[z], zz, c)

    def f_2_in(zz):
        return rc(fa1.at[zz], fag.at[zz], f2_s.at[zz], f2_r.at[zz], zz, c)

    def f_3(cc):
        return rc(fag.at[cc], fa3.at[c], f3_s.at[cc], f3_r.at[c], z, cc)

    def f_3_in(cc):
        return rc(fag.at[cc], fa3.at[cc], f3_s.at[cc], f3_r.at[cc], z, cc)

    shape_sq = (C2, C2)
    row_sq = lax.broadcasted_iota(jnp.int32, shape_sq, 0)
    col_sq = lax.broadcasted_iota(jnp.int32, shape_sq, 1)
    unmix = (row_sq == source_column(col_sq)).astype(F32).astype(BF)
    unmix_t = (col_sq == source_column(row_sq)).astype(F32).astype(BF)
    a_copy.wait()
    a_all = av[...].astype(F32)
    a_flat = jnp.concatenate([a_all[:, 0, :], a_all[:, 1, :]], axis=1).astype(BF)
    aint[...] = dot(a_flat, unmix).astype(BF)
    fas[...] = dot(unmix_t, a_flat, NT).astype(BF).reshape(8, 64, 128)

    for cc in cpeer:
        f_1(cc).start()
    fa1[c] = fas[c]

    def b_forward(zz):
        b_z_in(zz).wait_recv()
        for yy in ypeer:
            b_y(yy, zz).start()

    def cov_split(i):
        rows = pl.ds(pl.multiple_of(i * 128, 128), 128)
        hi, lo = split(cov[rows, :])
        chi[rows, :] = hi
        clo[rows, :] = lo
        for s in range(8):
            ccat[rows, s * 256:s * 256 + 128] = hi[:, s * 128:(s + 1) * 128]
            ccat[rows, s * 256 + 128:(s + 1) * 256] = lo[:, s * 128:(s + 1) * 128]
        pb[i] = jnp.zeros((C2, 128), F32)

    def w_split(i):
        rows = pl.ds(pl.multiple_of(i * 16, 16), 16)
        piece = wv[rows].astype(F32)
        wk[0, rows, :] = piece[:, 0, :].astype(BF)
        wk[1, rows, :] = piece[:, 1, :].astype(BF)

    cov_copy.wait()
    w_copy.wait()
    cov_split(0)
    w_split(0)

    @pl.loop(1, 8)
    def _(t):
        pl.when(z - t >= 0)(lambda: b_forward(z - t))
        pl.when(z + t <= 7)(lambda: b_forward(z + t))
        cov_split(t)
        w_split(t)

    b_c(y).start()

    for cc in cpeer:
        f_1_in(cc).wait_recv()
    for zz in zpeer:
        f_2(zz).start()
    fag[z] = fa1[z]

    row_i = lax.broadcasted_iota(jnp.int32, (128, 128), 0)
    col_i = lax.broadcasted_iota(jnp.int32, (128, 128), 1)
    pick = (col_i == ((row_i & 63) >> 3) * 16 + (row_i >> 6) * 8 + (row_i & 7)).astype(F32).astype(BF)

    def unpack(cc, yy):
        both = dot(pick, gat[cc, yy].reshape(128, 512)).astype(BF)
        rows = pl.ds(pl.multiple_of((cc * 4 + yy) * 64, 64), 64)
        ball[rows, 0:512] = both[0:64]
        ball[rows, 512:1024] = both[64:128]

    unpack(core, y)
    for yy in ypeer:
        for zz in zpeer + [z]:
            b_y_in(yy, zz).wait_recv()
        b_c(yy).start()
        unpack(core, yy)
    for yy in [y] + ypeer:
        b_c_in(yy).wait_recv()
        unpack(1 - core, yy)

    lane_k = (lax.broadcasted_iota(jnp.int32, (128, C2), 1) >> 2) & 1
    sub_k = (lax.broadcasted_iota(jnp.int32, (C2, 128), 0) >> 2) & 1

    proj = None
    for k in range(2):
        a_k = jnp.where(lane_k == k, aint[...].astype(F32), 0.0).astype(BF)
        diff = (wk[k].astype(F32) - dot(a_k, ball[...])).astype(BF)
        part = dot(ball[...], diff, NT)
        proj = part if k == 0 else jnp.where(sub_k == 1, part, proj)
    own = enc(proj)
    xg[z] = own

    def x_out(direction, s, q, zz):
        piece = xg.at[s, pl.ds(q * 128, 128)]
        return rc(piece, piece, xg_s.at[direction, s, q], xg_r.at[s, q], zz, c)

    for q in range(4):
        pl.when(z < 7)(lambda: x_out(0, z, q, up).start())
        pl.when(z > 0)(lambda: x_out(1, z, q, down).start())

    def x_decode(s, q):
        rows = pl.ds(q * 128, 128)
        lanes = pl.ds(pl.multiple_of(s * 128, 128), 128)
        hi, lo = split(dec(xg[s, rows]))
        xh[rows, lanes] = hi
        xl[rows, lanes] = lo

    def p_add(s, q):
        lanes = pl.ds(pl.multiple_of(s * 128, 128), 128)
        wide = pl.ds(pl.multiple_of(s * 256, 256), 256)
        hi = xh[:, lanes]
        c_hi = chi[q * 256:(q + 1) * 256, lanes]
        c_both = ccat[q * 256:(q + 1) * 256, wide]
        total = dot(jnp.concatenate([hi, hi], axis=1), c_both, NT) + dot(xl[:, lanes], c_hi, NT)
        total = total * (4.0 / O)
        pb[2 * q] = pb[2 * q] + total[:, 0:128]
        pb[2 * q + 1] = pb[2 * q + 1] + total[:, 128:256]

    for q in range(4):
        x_decode(z, q)

    @pl.loop(1, 8)
    def _(t):
        lo_s, hi_s = z - t, z + t
        for q in range(4):
            @pl.when(lo_s >= 0)
            def _():
                x_out(0, lo_s, q, up).wait_recv()
                pl.when(z < 7)(lambda: x_out(0, lo_s, q, up).start())

            @pl.when(hi_s <= 7)
            def _():
                x_out(1, hi_s, q, down).wait_recv()
                pl.when(z > 0)(lambda: x_out(1, hi_s, q, down).start())

            pl.when(lo_s >= 0)(lambda: x_decode(lo_s, q))
            pl.when(hi_s <= 7)(lambda: x_decode(hi_s, q))
            pl.when(lo_s + 1 >= 0)(lambda: p_add(lo_s + 1, q))
            pl.when(jnp.logical_and(t > 1, hi_s - 1 <= 7))(lambda: p_add(hi_s - 1, q))

        @pl.when(t == 2)
        def _():
            for zz in zpeer:
                f_2_in(zz).wait_recv()
            for cc in cpeer:
                f_3(cc).start()
            fa3[c] = fag[c]

    for q in range(4):
        pl.when(z == 7)(lambda: p_add(0, q))
        pl.when(z == 0)(lambda: p_add(7, q))

    def cols(h):
        return pl.ds(h * 256, 256)

    def p_c(h, yy):
        return rc(pes.at[yy, cols(h)], per_.at[yy, cols(h)], pc_s.at[h, yy], pc_r.at[h, yy], z, other)

    def p_y(h, yy):
        return rc(ses.at[yy, cols(h)], ser.at[y, cols(h)], ps_s.at[h, yy], ps_r.at[h, y], z, 2 * yy + core)

    def p_y_in(h, yy):
        return rc(ses.at[yy, cols(h)], ser.at[yy, cols(h)], ps_s.at[h, yy], ps_r.at[h, yy], z, 2 * yy + core)

    def p_core(h):
        for yy in ypeer + [y]:
            pes[yy, cols(h)] = enc(pb[2 * yy + 1 - core, cols(h)])
            p_c(h, yy).start()

    def p_plane(h):
        for yy in ypeer:
            p_c(h, yy).wait_recv()
            ses[yy, cols(h)] = enc(pb[2 * yy + core, cols(h)] + dec(per_[yy, cols(h)]))
            p_y(h, yy).start()

    def eighths(h):
        return pl.ds(4 * h, 4)

    def n_y(h, yy):
        piece = nag.at[c, eighths(h)]
        return rc(piece, piece, ny_s.at[h, yy], ng_r.at[h, c], z, 2 * yy + core)

    def n_c(h, yy):
        piece = nag.at[2 * yy + core, eighths(h)]
        return rc(piece, piece, nc_s.at[h, yy], ng_r.at[h, 2 * yy + core], z, other)

    def n_in(h, j):
        piece = nag.at[j, eighths(h)]
        return rc(piece, piece, nc_s.at[h, 0], ng_r.at[h, j], z, other)

    def p_end(h):
        p_c(h, y).wait_recv()
        new_a = pb[c, cols(h)] + dec(per_[y, cols(h)])
        for yy in ypeer:
            p_y_in(h, yy).wait_recv()
            new_a = new_a + dec(ser[yy, cols(h)])
        if h == 0:
            for cc in cpeer:
                f_3_in(cc).wait_recv()
        new_a = new_a + fa3[eighths(h)].reshape(256, 128).astype(F32)
        nag[c, eighths(h)] = enc(new_a).reshape(4, 64, 128)
        for yy in ypeer:
            n_y(h, yy).start()
        n_c(h, y).start()

    p_core(0)
    p_core(1)
    p_plane(0)
    p_plane(1)
    p_end(0)
    p_end(1)

    def t_z(zz):
        return rc(nag.at[zz, c], tz.at[z], tz_s.at[zz], tz_r.at[z], zz, c)

    def t_z_in(zz):
        return rc(nag.at[zz, c], tz.at[zz], tz_s.at[zz], tz_r.at[zz], zz, c)

    def t_n(r):
        return rc(tz.at[r], tn.at[c], tn_s.at[r], tn_r.at[c], z, r)

    def t_n_in(r):
        return rc(tz.at[r], tn.at[r], tn_s.at[r], tn_r.at[r], z, r)

    def n_take(j, h):
        if h == 1:
            pl.when(j != z)(lambda: t_z(j).start())
        lanes = pl.ds(pl.multiple_of(j * 128, 128), 128)
        hi, lo = split(dec(nag[j, eighths(h)].reshape(256, 128)))
        xh[cols(h), lanes] = hi
        xl[cols(h), lanes] = lo

    def f_add(yy, h, first=False):
        pair = pl.ds(pl.multiple_of(yy * 256, 256), 256)
        rows = cols(h)

        @pl.loop(0, 4)
        def _(i):
            lanes = pl.ds(pl.multiple_of(i * 256, 256), 256)
            c_hi = chi[pair, lanes]
            total = dot(xh[rows, pair], c_hi) + dot(xl[rows, pair], c_hi) + dot(xh[rows, pair], clo[pair, lanes])
            total = total * FIELD_DOWN
            if first:
                fb[2 * i, rows] = total[:, 0:128]
                fb[2 * i + 1, rows] = total[:, 128:256]
            else:
                fb[2 * i, rows] = fb[2 * i, rows] + total[:, 0:128]
                fb[2 * i + 1, rows] = fb[2 * i + 1, rows] + total[:, 128:256]

    def n_near(yy, h):
        n_in(h, 2 * yy + core).wait_recv()
        n_c(h, yy).start()
        n_take(2 * yy + core, h)

    def n_far(yy, h):
        n_in(h, 2 * yy + 1 - core).wait_recv()
        n_take(2 * yy + 1 - core, h)

    def second(h):
        n_take(c, h)
        n_far(y, h)
        f_add(y, h, True)
        n_near(ypeer[0], h)
        n_near(ypeer[1], h)
        n_far(ypeer[0], h)
        f_add(ypeer[0], h)
        n_near(ypeer[2], h)
        n_far(ypeer[1], h)
        f_add(ypeer[1], h)
        n_far(ypeer[2], h)
        f_add(ypeer[2], h)

    def z_out(direction, d, q, zz):
        rows = pl.ds(q * 128, 128)
        return rc(
            zs.at[direction, d, rows], zr.at[direction, d, rows],
            zr_s.at[direction, d, q], zr_r.at[direction, d, q], zz, c,
        )

    def z_move(direction, d, q, first, last, zz):
        rows = pl.ds(q * 128, 128)

        @pl.when(jnp.logical_and(first, jnp.logical_not(last)))
        def _():
            zs[direction, d, rows] = enc(fb[d, rows])

        @pl.when(jnp.logical_not(first))
        def _():
            z_out(direction, d, q, zz).wait_recv()
            total = fb[d, rows] + dec(zr[direction, d, rows])

            @pl.when(last)
            def _():
                fb[d, rows] = total

            @pl.when(jnp.logical_not(last))
            def _():
                zs[direction, d, rows] = enc(total)

        @pl.when(jnp.logical_not(last))
        def _():
            z_out(direction, d, q, zz).start()

    def z_step(t, h):
        for q in (2 * h, 2 * h + 1):
            pl.when(t >= z)(lambda: z_move(0, 7 + z - t, q, z == 0, t == 7, up))
            pl.when(t >= 7 - z)(lambda: z_move(1, t - 7 + z, q, z == 7, t == 7, down))

    def natural():
        rows_a = dec(tn[...].reshape(C2, 128)).T
        hi, lo = split(rows_a)
        return rows_a, hi, lo

    def second_difference(k):
        _, hi, lo = natural()
        hi_k = jnp.where(lane_k == k, hi.astype(F32), 0.0).astype(BF)
        lo_k = jnp.where(lane_k == k, lo.astype(F32), 0.0).astype(BF)
        fit = dot(hi_k, ball[...]) + dot(lo_k, ball[...])
        d2[k * 128:(k + 1) * 128, :] = (wk[k].astype(F32) - fit).astype(BF)

    second(0)
    z_step(0, 0)
    second(1)
    tz[z] = nag[z, c]

    @pl.loop(0, 7)
    def _(t):
        z_step(t + 1, 0)
        z_step(t, 1)

        @pl.when(t == 3)
        def _():
            for zz in zpeer:
                t_z_in(zz).wait_recv()
            for r in cpeer:
                t_n(r).start()
            tn[c] = tz[c]

        @pl.when(t == 5)
        def _():
            for r in cpeer:
                t_n_in(r).wait_recv()
            second_difference(0)

        @pl.when(t == 6)
        def _():
            second_difference(1)

    z_step(7, 1)

    field = fb[z] * (FIELD_UP * 8.0 / D)
    wide = jnp.concatenate([jnp.where(sub_k == 0, field, 0.0), jnp.where(sub_k == 1, field, 0.0)], axis=1)
    hi, lo = split(wide)
    xh[:, 0:256] = hi
    xl[:, 0:256] = lo

    def f_c(h):
        return rc(fcs.at[h], fcr.at[h], fc_s.at[h], fc_r.at[h], z, other)

    def f_y(h, yy):
        return rc(fys.at[h, yy], fyr.at[h, y], fy_s.at[h, yy], fy_r.at[h, y], z, 2 * yy + core)

    def f_y_in(h, yy):
        return rc(fys.at[h, yy], fyr.at[h, yy], fy_s.at[h, yy], fy_r.at[h, yy], z, 2 * yy + core)

    def f_z(h, zz):
        return rc(fzs.at[h, zz], fzr.at[h, z], fz_s.at[h, zz], fz_r.at[h, z], zz, c)

    def f_z_in(h, zz):
        return rc(fzs.at[h, zz], fzr.at[h, zz], fz_s.at[h, zz], fz_r.at[h, zz], zz, c)

    def half(which, h):
        rows = pl.ds(pl.multiple_of(which * 256, 256), 256)
        right = d2[:, h * 512:(h + 1) * 512]
        return (dot(xh[rows, 0:256], right) + dot(xl[rows, 0:256], right)).reshape(4, 64, 512)

    for h in range(2):
        fcs[h] = enc(half(1 - core, h))
        f_c(h).start()
    for h in range(2):
        p2[h] = half(core, h)
        f_c(h).wait_recv()
        for yy in ypeer:
            fys[h, yy] = enc(p2[h, yy] + dec(fcr[h, yy]))
            f_y(h, yy).start()
    rows_a, hi, lo = natural()
    lo2 = (rows_a - hi.astype(F32) - lo.astype(F32)).astype(BF)
    back = (lax.broadcasted_iota(jnp.int32, shape_sq, 0) == source_column(lax.broadcasted_iota(jnp.int32, shape_sq, 1))).astype(F32).astype(BF)
    na_ref[...] = dot(hi, back, NT) + dot(lo, back, NT) + dot(lo2, back, NT)
    for h in range(2):
        total = p2[h, y] + dec(fcr[h, y])
        for yy in ypeer:
            f_y_in(h, yy).wait_recv()
            total = total + dec(fyr[h, yy])
        fsum[h] = total.reshape(8, 8, 512)
        for zz in zpeer:
            mine = fsum[h, zz]
            fzs[h, zz] = enc(jnp.concatenate([mine[:, 0:256], mine[:, 256:512]], axis=0))
            f_z(h, zz).start()
    for h in range(2):
        rest = None
        for zz in zpeer:
            f_z_in(h, zz).wait_recv()
            got = dec(fzr[h, zz])
            rest = got if rest is None else rest + got
        gained = fsum[h, z] + jnp.concatenate([rest[0:8], rest[8:16]], axis=1)
        nb_ref[:, h * 512:(h + 1) * 512] = b_own[:, h * 512:(h + 1) * 512] + gained

    for zz in zpeer:
        b_z(zz).wait_send()
        f_2(zz).wait_send()
        t_z(zz).wait_send()
        for h in range(2):
            f_z(h, zz).wait_send()
        for yy in ypeer:
            b_y(yy, zz).wait_send()
    for r in cpeer:
        t_n(r).wait_send()
        f_1(r).wait_send()
        f_3(r).wait_send()
    for yy in ypeer:
        b_y(yy, z).wait_send()
        for h in range(2):
            p_y(h, yy).wait_send()
            n_y(h, yy).wait_send()
            f_y(h, yy).wait_send()
    for yy in ypeer + [y]:
        b_c(yy).wait_send()
        for h in range(2):
            p_c(h, yy).wait_send()
            n_c(h, yy).wait_send()
    for h in range(2):
        f_c(h).wait_send()

    @pl.loop(0, 8)
    def _(s):
        for q in range(4):
            pl.when(jnp.logical_and(s <= z, z < 7))(lambda: x_out(0, s, q, up).wait_send())
            pl.when(jnp.logical_and(s >= z, z > 0))(lambda: x_out(1, s, q, down).wait_send())
            pl.when(s > z)(lambda: z_out(0, s, q, up).wait_send())
            pl.when(s < z)(lambda: z_out(1, s, q, down).wait_send())


def per_device(covariance, weight, factor_a, factor_b):
    n = weight.shape[0]
    vm = pl.BlockSpec(memory_space=pltpu.VMEM)
    blk = (8, C2, 128)
    dma = pltpu.SemaphoreType.DMA
    new_a, new_b = pl.pallas_call(
        kernel,
        name="refine",
        out_shape=(jax.ShapeDtypeStruct((n, C2), F32), jax.ShapeDtypeStruct((8, O), F32)),
        in_specs=[pl.BlockSpec(memory_space=pl.ANY)] * 3 + [vm],
        out_specs=(vm, vm),
        scratch_shapes=[
            pltpu.VMEM((1024, 1024), F32),
            pltpu.VMEM((n, 2, O), BF),
            pltpu.VMEM((n, 2, R), BF),
            pltpu.VMEM((2, n, O), BF),
            pltpu.VMEM((1024, 1024), BF),
            pltpu.VMEM((1024, 1024), BF),
            pltpu.VMEM((1024, 2048), BF),
            pltpu.VMEM((2, 4, 8, 16, 512), BF),
            pltpu.VMEM((C2, O), BF),
            pltpu.VMEM((128, C2), BF),
            pltpu.VMEM(blk, BF),
            pltpu.VMEM((C2, 1024), BF),
            pltpu.VMEM((C2, 1024), BF),
            pltpu.VMEM((8, 64, 128), BF),
            pltpu.VMEM((8, 64, 128), BF),
            pltpu.VMEM((8, 64, 128), BF),
            pltpu.VMEM((8, 64, 128), BF),
            pltpu.VMEM(blk, F32),
            pltpu.VMEM((4, C2, 128), BF),
            pltpu.VMEM((4, C2, 128), BF),
            pltpu.VMEM((4, C2, 128), BF),
            pltpu.VMEM((4, C2, 128), BF),
            pltpu.VMEM((8, 8, 64, 128), BF),
            pltpu.VMEM((8, 64, 128), BF),
            pltpu.VMEM((8, 64, 128), BF),
            pltpu.VMEM(blk, F32),
            pltpu.VMEM((2,) + blk, BF),
            pltpu.VMEM((2,) + blk, BF),
            pltpu.VMEM((256, O), BF),
            pltpu.VMEM((2, 4, 64, 512), F32),
            pltpu.VMEM((2, 4, 64, 512), BF),
            pltpu.VMEM((2, 4, 64, 512), BF),
            pltpu.VMEM((2, 4, 64, 512), BF),
            pltpu.VMEM((2, 4, 64, 512), BF),
            pltpu.VMEM((2, 8, 8, 512), F32),
            pltpu.VMEM((2, 8, 16, 256), BF),
            pltpu.VMEM((2, 8, 16, 256), BF),
            dma, dma, dma,
            dma((8,)), dma((8,)), dma((4, 8)), dma((4, 8)), dma((4,)), dma((4,)),
            dma((8,)), dma((8,)), dma((8,)), dma((8,)), dma((8,)), dma((8,)),
            dma((2, 8, 4)), dma((8, 4)),
            dma((2, 4)), dma((2, 4)), dma((2, 4)), dma((2, 4)),
            dma((2, 4)), dma((2, 4)), dma((2, 8)),
            dma((8,)), dma((8,)), dma((8,)), dma((8,)),
            dma((2, 8, 4)), dma((2, 8, 4)),
            dma((2,)), dma((2,)), dma((2, 4)), dma((2, 4)), dma((2, 8)), dma((2, 8)),
        ],
        compiler_params=pltpu.CompilerParams(
            collective_id=0, has_side_effects=True, vmem_limit_bytes=56 * 2**20
        ),
    )(covariance, weight, factor_a, factor_b)
    return new_a.reshape(n, 2, R), new_b.reshape(2, 4, O)


def solution(mesh):
    in_specs = (
        P(("layer", "row"), "col"),
        P(("layer", "col", "row"), None, None),
        P(("layer", "col", "row"), None, None),
        P("layer", ("row", "col"), None),
    )
    out_specs = (P(("layer", "col", "row"), None, None), P("layer", ("row", "col"), None))
    return jax.shard_map(
        per_device, mesh=mesh, in_specs=in_specs, out_specs=out_specs, check_vma=False
    )
```

```python
import functools

import jax
import jax.numpy as jnp
from jax import lax
from jax.experimental import pallas as pl
from jax.experimental.pallas import tpu as pltpu
from jax.sharding import PartitionSpec as P

MESH = pl.DeviceIdType.MESH
F32 = jnp.float32
BF = jnp.bfloat16
D = 8192
O = 1024
R = 256
C2 = 2 * R
FIELD_DOWN = 1.0 / 256.0
FIELD_UP = 256.0

NN = (((1,), (0,)), ((), ()))
NT = (((1,), (1,)), ((), ()))


def enc(x):
    s = x * x
    s = s * s
    return jnp.where(x < 0, -s, s).astype(BF)


def dec(v):
    f = v.astype(F32)
    r = jnp.sqrt(jnp.sqrt(jnp.abs(f)))
    return jnp.where(f < 0, -r, r)


def split(x):
    hi = x.astype(BF)
    return hi, (x - hi.astype(F32)).astype(BF)


def dot(a, b, dims=NN):
    return lax.dot_general(a, b, dims, preferred_element_type=F32)


def source_column(i):
    core = i >> 8
    y = (i >> 6) & 3
    z = (i >> 3) & 7
    k = (i >> 2) & 1
    return k * R + 4 * (z * 8 + y * 2 + core) + (i & 3)


def kernel(
    cov_hbm, w_hbm, a_hbm, b_ref, na_ref, nb_ref,
    cov, wv, av, wk, chi, clo, ccat, gat, ball, aint, xg, xh, xl, fas, fa1, fag, fa3, pb, pes, per_, ses, ser,
    nag, tz, tn, fb, zs, zr, d2, p2, fcs, fcr, fys, fyr, fsum, fzs, fzr,
    cov_sem, w_sem, a_sem, bz_s, bz_r, by_s, by_r, bc_s, bc_r, f1_s, f1_r, f2_s, f2_r, f3_s, f3_r, xg_s, xg_r,
    pc_s, pc_r, ps_s, ps_r, ny_s, nc_s, ng_r, tz_s, tz_r, tn_s, tn_r, zr_s, zr_r,
    fc_s, fc_r, fy_s, fy_r, fz_s, fz_r,
):
    layer = lax.axis_index("layer")
    z = lax.axis_index("row")
    c = lax.axis_index("col")
    y = lax.div(c, 2)
    core = lax.rem(c, 2)
    other = c + 1 - 2 * core
    up, down = lax.rem(z + 1, 8), lax.rem(z + 7, 8)

    def rc(src, dst, ss, rs, zz, cc):
        return pltpu.make_async_remote_copy(
            src_ref=src, dst_ref=dst, send_sem=ss, recv_sem=rs,
            device_id=(layer, zz, cc), device_id_type=MESH,
        )

    cov_copy = pltpu.make_async_copy(cov_hbm, cov, cov_sem)
    w_copy = pltpu.make_async_copy(w_hbm, wv, w_sem)
    a_copy = pltpu.make_async_copy(a_hbm, av, a_sem)
    a_copy.start()
    cov_copy.start()
    w_copy.start()

    zpeer = [lax.rem(z + d, 8) for d in (1, 7, 2, 6, 3, 5, 4)]
    ypeer = [lax.rem(y + d, 4) for d in (1, 3, 2)]
    cpeer = [lax.rem(c + d, 8) for d in range(1, 8)]

    barrier = pltpu.get_barrier_semaphore()
    for zz in zpeer:
        pl.semaphore_signal(barrier, inc=1, device_id=(layer, zz, c), device_id_type=MESH)
    for cc in cpeer:
        pl.semaphore_signal(barrier, inc=1, device_id=(layer, z, cc), device_id_type=MESH)

    b_own = b_ref[...].astype(F32)
    b_own = jnp.concatenate([b_own[0], b_own[1]], axis=0)
    gat[core, y, z] = jnp.concatenate([b_own[:, 0:512], b_own[:, 512:1024]], axis=0).astype(BF)

    pl.semaphore_wait(barrier, 14)

    def b_z(zz):
        return rc(gat.at[core, y, z], gat.at[core, y, z], bz_s.at[zz], bz_r.at[z], zz, c)

    def b_z_in(zz):
        return rc(gat.at[core, y, zz], gat.at[core, y, zz], bz_s.at[zz], bz_r.at[zz], zz, c)

    def b_y(yy, zz):
        return rc(gat.at[core, y, zz], gat.at[core, y, zz], by_s.at[yy, zz], by_r.at[y, zz], z, 2 * yy + core)

    def b_y_in(yy, zz):
        return rc(gat.at[core, yy, zz], gat.at[core, yy, zz], by_s.at[yy, zz], by_r.at[yy, zz], z, 2 * yy + core)

    def b_c(yy):
        return rc(gat.at[core, yy], gat.at[core, yy], bc_s.at[yy], bc_r.at[yy], z, other)

    def b_c_in(yy):
        return rc(gat.at[1 - core, yy], gat.at[1 - core, yy], bc_s.at[yy], bc_r.at[yy], z, other)

    for zz in zpeer:
        b_z(zz).start()
    for yy in ypeer:
        b_y(yy, z).start()

    def f_1(cc):
        return rc(fas.at[cc], fa1.at[c], f1_s.at[cc], f1_r.at[c], z, cc)

    def f_1_in(cc):
        return rc(fas.at[cc], fa1.at[cc], f1_s.at[cc], f1_r.at[cc], z, cc)

    def f_2(zz):
        return rc(fa1.at[zz], fag.at[z], f2_s.at[zz], f2_r.at[z], zz, c)

    def f_2_in(zz):
        return rc(fa1.at[zz], fag.at[zz], f2_s.at[zz], f2_r.at[zz], zz, c)

    def f_3(cc):
        return rc(fag.at[cc], fa3.at[c], f3_s.at[cc], f3_r.at[c], z, cc)

    def f_3_in(cc):
        return rc(fag.at[cc], fa3.at[cc], f3_s.at[cc], f3_r.at[cc], z, cc)

    shape_sq = (C2, C2)
    row_sq = lax.broadcasted_iota(jnp.int32, shape_sq, 0)
    col_sq = lax.broadcasted_iota(jnp.int32, shape_sq, 1)
    unmix = (row_sq == source_column(col_sq)).astype(F32).astype(BF)
    unmix_t = (col_sq == source_column(row_sq)).astype(F32).astype(BF)
    a_copy.wait()
    a_all = av[...].astype(F32)
    a_flat = jnp.concatenate([a_all[:, 0, :], a_all[:, 1, :]], axis=1).astype(BF)
    aint[...] = dot(a_flat, unmix).astype(BF)
    fas[...] = dot(unmix_t, a_flat, NT).astype(BF).reshape(8, 64, 128)

    for cc in cpeer:
        f_1(cc).start()
    fa1[c] = fas[c]

    def b_forward(zz):
        b_z_in(zz).wait_recv()
        for yy in ypeer:
            b_y(yy, zz).start()

    def cov_split(i):
        rows = pl.ds(pl.multiple_of(i * 128, 128), 128)
        hi, lo = split(cov[rows, :])
        chi[rows, :] = hi
        clo[rows, :] = lo
        for s in range(8):
            ccat[rows, s * 256:s * 256 + 128] = hi[:, s * 128:(s + 1) * 128]
            ccat[rows, s * 256 + 128:(s + 1) * 256] = lo[:, s * 128:(s + 1) * 128]
        pb[i] = jnp.zeros((C2, 128), F32)

    def w_split(i):
        rows = pl.ds(pl.multiple_of(i * 16, 16), 16)
        piece = wv[rows].astype(F32)
        wk[0, rows, :] = piece[:, 0, :].astype(BF)
        wk[1, rows, :] = piece[:, 1, :].astype(BF)

    cov_copy.wait()
    w_copy.wait()
    cov_split(0)
    w_split(0)

    @pl.loop(1, 8)
    def _(t):
        pl.when(z - t >= 0)(lambda: b_forward(z - t))
        pl.when(z + t <= 7)(lambda: b_forward(z + t))
        cov_split(t)
        w_split(t)

    b_c(y).start()

    for cc in cpeer:
        f_1_in(cc).wait_recv()
    for zz in zpeer:
        f_2(zz).start()
    fag[z] = fa1[z]

    row_i = lax.broadcasted_iota(jnp.int32, (128, 128), 0)
    col_i = lax.broadcasted_iota(jnp.int32, (128, 128), 1)
    pick = (col_i == ((row_i & 63) >> 3) * 16 + (row_i >> 6) * 8 + (row_i & 7)).astype(F32).astype(BF)

    def unpack(cc, yy):
        both = dot(pick, gat[cc, yy].reshape(128, 512)).astype(BF)
        rows = pl.ds(pl.multiple_of((cc * 4 + yy) * 64, 64), 64)
        ball[rows, 0:512] = both[0:64]
        ball[rows, 512:1024] = both[64:128]

    unpack(core, y)
    for yy in ypeer:
        for zz in zpeer + [z]:
            b_y_in(yy, zz).wait_recv()
        b_c(yy).start()
        unpack(core, yy)
    for yy in [y] + ypeer:
        b_c_in(yy).wait_recv()
        unpack(1 - core, yy)

    lane_k = (lax.broadcasted_iota(jnp.int32, (128, C2), 1) >> 2) & 1
    sub_k = (lax.broadcasted_iota(jnp.int32, (C2, 128), 0) >> 2) & 1

    proj = None
    for k in range(2):
        a_k = jnp.where(lane_k == k, aint[...].astype(F32), 0.0).astype(BF)
        diff = (wk[k].astype(F32) - dot(a_k, ball[...])).astype(BF)
        part = dot(ball[...], diff, NT)
        proj = part if k == 0 else jnp.where(sub_k == 1, part, proj)
    own = enc(proj)
    xg[z] = own

    def x_out(direction, s, q, zz):
        piece = xg.at[s, pl.ds(q * 128, 128)]
        return rc(piece, piece, xg_s.at[direction, s, q], xg_r.at[s, q], zz, c)

    for q in range(4):
        pl.when(z < 7)(lambda: x_out(0, z, q, up).start())
        pl.when(z > 0)(lambda: x_out(1, z, q, down).start())

    def x_decode(s, q):
        rows = pl.ds(q * 128, 128)
        lanes = pl.ds(pl.multiple_of(s * 128, 128), 128)
        hi, lo = split(dec(xg[s, rows]))
        xh[rows, lanes] = hi
        xl[rows, lanes] = lo

    def p_add(s, q):
        lanes = pl.ds(pl.multiple_of(s * 128, 128), 128)
        wide = pl.ds(pl.multiple_of(s * 256, 256), 256)
        hi = xh[:, lanes]
        c_hi = chi[q * 256:(q + 1) * 256, lanes]
        c_both = ccat[q * 256:(q + 1) * 256, wide]
        total = dot(jnp.concatenate([hi, hi], axis=1), c_both, NT) + dot(xl[:, lanes], c_hi, NT)
        total = total * (4.0 / O)
        pb[2 * q] = pb[2 * q] + total[:, 0:128]
        pb[2 * q + 1] = pb[2 * q + 1] + total[:, 128:256]

    def p_rows(s, q):
        rows = pl.ds(q * 128, 128)
        lanes = pl.ds(pl.multiple_of(s * 128, 128), 128)
        wide = pl.ds(pl.multiple_of(s * 256, 256), 256)
        hi = xh[rows, lanes]
        both = jnp.concatenate([hi, hi], axis=1)
        low = xl[rows, lanes]
        for i in range(4):
            part = pl.ds(i * 256, 256)
            total = dot(both, ccat[part, wide], NT) + dot(low, chi[part, lanes], NT)
            total = total * (4.0 / O)
            pb[2 * i, rows] = pb[2 * i, rows] + total[:, 0:128]
            pb[2 * i + 1, rows] = pb[2 * i + 1, rows] + total[:, 128:256]

    for q in range(4):
        x_decode(z, q)

    @pl.loop(1, 7)
    def _(t):
        lo_s, hi_s = z - t, z + t
        for q in range(4):
            @pl.when(lo_s >= 0)
            def _():
                x_out(0, lo_s, q, up).wait_recv()
                pl.when(z < 7)(lambda: x_out(0, lo_s, q, up).start())

            @pl.when(hi_s <= 7)
            def _():
                x_out(1, hi_s, q, down).wait_recv()
                pl.when(z > 0)(lambda: x_out(1, hi_s, q, down).start())

            pl.when(lo_s >= 0)(lambda: x_decode(lo_s, q))
            pl.when(hi_s <= 7)(lambda: x_decode(hi_s, q))
            pl.when(lo_s + 1 >= 0)(lambda: p_add(lo_s + 1, q))
            pl.when(jnp.logical_and(t > 1, hi_s - 1 <= 7))(lambda: p_add(hi_s - 1, q))

        @pl.when(t == 2)
        def _():
            for zz in zpeer:
                f_2_in(zz).wait_recv()
            for cc in cpeer:
                f_3(cc).start()
            fa3[c] = fag[c]

    for q in range(4):
        pl.when(z >= 6)(lambda: p_add(z - 6, q))
        pl.when(z <= 1)(lambda: p_add(z + 6, q))

    def x_last(q):
        @pl.when(jnp.logical_or(z == 0, z == 7))
        def _():
            x_out(0, 7 - z, q, up).wait_recv()
            x_decode(7 - z, q)
            p_rows(7 - z, q)

    def cols(h):
        return pl.ds(h * 256, 256)

    def p_c(h, yy):
        return rc(pes.at[yy, cols(h)], per_.at[yy, cols(h)], pc_s.at[h, yy], pc_r.at[h, yy], z, other)

    def p_y(h, yy):
        return rc(ses.at[yy, cols(h)], ser.at[y, cols(h)], ps_s.at[h, yy], ps_r.at[h, y], z, 2 * yy + core)

    def p_y_in(h, yy):
        return rc(ses.at[yy, cols(h)], ser.at[yy, cols(h)], ps_s.at[h, yy], ps_r.at[h, yy], z, 2 * yy + core)

    def p_core(h):
        for yy in ypeer + [y]:
            pes[yy, cols(h)] = enc(pb[2 * yy + 1 - core, cols(h)])
            p_c(h, yy).start()

    def p_plane(h):
        for yy in ypeer:
            p_c(h, yy).wait_recv()
            ses[yy, cols(h)] = enc(pb[2 * yy + core, cols(h)] + dec(per_[yy, cols(h)]))
            p_y(h, yy).start()

    def eighths(h):
        return pl.ds(4 * h, 4)

    def n_y(h, yy):
        piece = nag.at[c, eighths(h)]
        return rc(piece, piece, ny_s.at[h, yy], ng_r.at[h, c], z, 2 * yy + core)

    def n_c(h, yy):
        piece = nag.at[2 * yy + core, eighths(h)]
        return rc(piece, piece, nc_s.at[h, yy], ng_r.at[h, 2 * yy + core], z, other)

    def n_in(h, j):
        piece = nag.at[j, eighths(h)]
        return rc(piece, piece, nc_s.at[h, 0], ng_r.at[h, j], z, other)

    def p_end(h):
        p_c(h, y).wait_recv()
        new_a = pb[c, cols(h)] + dec(per_[y, cols(h)])
        for yy in ypeer:
            p_y_in(h, yy).wait_recv()
            new_a = new_a + dec(ser[yy, cols(h)])
        if h == 0:
            for cc in cpeer:
                f_3_in(cc).wait_recv()
        new_a = new_a + fa3[eighths(h)].reshape(256, 128).astype(F32)
        nag[c, eighths(h)] = enc(new_a).reshape(4, 64, 128)
        for yy in ypeer:
            n_y(h, yy).start()
        n_c(h, y).start()

    x_last(0)
    x_last(1)
    p_core(0)
    x_last(2)
    p_plane(0)
    x_last(3)
    p_core(1)
    p_plane(1)
    p_end(0)
    p_end(1)

    def t_z(zz):
        return rc(nag.at[zz, c], tz.at[z], tz_s.at[zz], tz_r.at[z], zz, c)

    def t_z_in(zz):
        return rc(nag.at[zz, c], tz.at[zz], tz_s.at[zz], tz_r.at[zz], zz, c)

    def t_n(r):
        return rc(tz.at[r], tn.at[c], tn_s.at[r], tn_r.at[c], z, r)

    def t_n_in(r):
        return rc(tz.at[r], tn.at[r], tn_s.at[r], tn_r.at[r], z, r)

    def n_take(j, h):
        if h == 1:
            pl.when(j != z)(lambda: t_z(j).start())
        lanes = pl.ds(pl.multiple_of(j * 128, 128), 128)
        hi, lo = split(dec(nag[j, eighths(h)].reshape(256, 128)))
        xh[cols(h), lanes] = hi
        xl[cols(h), lanes] = lo

    def f_add(yy, h, first=False):
        pair = pl.ds(pl.multiple_of(yy * 256, 256), 256)
        rows = cols(h)

        @pl.loop(0, 4)
        def _(i):
            lanes = pl.ds(pl.multiple_of(i * 256, 256), 256)
            c_hi = chi[pair, lanes]
            total = dot(xh[rows, pair], c_hi) + dot(xl[rows, pair], c_hi) + dot(xh[rows, pair], clo[pair, lanes])
            total = total * FIELD_DOWN
            if first:
                fb[2 * i, rows] = total[:, 0:128]
                fb[2 * i + 1, rows] = total[:, 128:256]
            else:
                fb[2 * i, rows] = fb[2 * i, rows] + total[:, 0:128]
                fb[2 * i + 1, rows] = fb[2 * i + 1, rows] + total[:, 128:256]

    def n_near(yy, h):
        n_in(h, 2 * yy + core).wait_recv()
        n_c(h, yy).start()
        n_take(2 * yy + core, h)

    def n_far(yy, h):
        n_in(h, 2 * yy + 1 - core).wait_recv()
        n_take(2 * yy + 1 - core, h)

    def second(h):
        n_take(c, h)
        n_far(y, h)
        f_add(y, h, True)
        n_near(ypeer[0], h)
        n_near(ypeer[1], h)
        n_far(ypeer[0], h)
        f_add(ypeer[0], h)
        n_near(ypeer[2], h)
        n_far(ypeer[1], h)
        f_add(ypeer[1], h)
        n_far(ypeer[2], h)
        f_add(ypeer[2], h)

    def z_out(direction, d, q, zz):
        rows = pl.ds(q * 128, 128)
        return rc(
            zs.at[direction, d, rows], zr.at[direction, d, rows],
            zr_s.at[direction, d, q], zr_r.at[direction, d, q], zz, c,
        )

    def z_move(direction, d, q, first, last, zz):
        rows = pl.ds(q * 128, 128)

        @pl.when(jnp.logical_and(first, jnp.logical_not(last)))
        def _():
            zs[direction, d, rows] = enc(fb[d, rows])

        @pl.when(jnp.logical_not(first))
        def _():
            z_out(direction, d, q, zz).wait_recv()
            total = fb[d, rows] + dec(zr[direction, d, rows])

            @pl.when(last)
            def _():
                fb[d, rows] = total

            @pl.when(jnp.logical_not(last))
            def _():
                zs[direction, d, rows] = enc(total)

        @pl.when(jnp.logical_not(last))
        def _():
            z_out(direction, d, q, zz).start()

    def z_step(t, h):
        for q in (2 * h, 2 * h + 1):
            pl.when(t >= z)(lambda: z_move(0, 7 + z - t, q, z == 0, t == 7, up))
            pl.when(t >= 7 - z)(lambda: z_move(1, t - 7 + z, q, z == 7, t == 7, down))

    def natural():
        rows_a = dec(tn[...].reshape(C2, 128)).T
        hi, lo = split(rows_a)
        return rows_a, hi, lo

    def second_difference(k):
        _, hi, lo = natural()
        hi_k = jnp.where(lane_k == k, hi.astype(F32), 0.0).astype(BF)
        lo_k = jnp.where(lane_k == k, lo.astype(F32), 0.0).astype(BF)
        fit = dot(hi_k, ball[...]) + dot(lo_k, ball[...])
        d2[k * 128:(k + 1) * 128, :] = (wk[k].astype(F32) - fit).astype(BF)

    second(0)
    z_step(0, 0)
    second(1)
    tz[z] = nag[z, c]

    @pl.loop(0, 7)
    def _(t):
        z_step(t + 1, 0)
        z_step(t, 1)

        @pl.when(t == 3)
        def _():
            for zz in zpeer:
                t_z_in(zz).wait_recv()
            for r in cpeer:
                t_n(r).start()
            tn[c] = tz[c]

        @pl.when(t == 5)
        def _():
            for r in cpeer:
                t_n_in(r).wait_recv()
            second_difference(0)

        @pl.when(t == 6)
        def _():
            second_difference(1)

    z_step(7, 1)

    field = fb[z] * (FIELD_UP * 8.0 / D)
    wide = jnp.concatenate([jnp.where(sub_k == 0, field, 0.0), jnp.where(sub_k == 1, field, 0.0)], axis=1)
    hi, lo = split(wide)
    xh[:, 0:256] = hi
    xl[:, 0:256] = lo

    def f_c(h):
        return rc(fcs.at[h], fcr.at[h], fc_s.at[h], fc_r.at[h], z, other)

    def f_y(h, yy):
        return rc(fys.at[h, yy], fyr.at[h, y], fy_s.at[h, yy], fy_r.at[h, y], z, 2 * yy + core)

    def f_y_in(h, yy):
        return rc(fys.at[h, yy], fyr.at[h, yy], fy_s.at[h, yy], fy_r.at[h, yy], z, 2 * yy + core)

    def f_z(h, zz):
        return rc(fzs.at[h, zz], fzr.at[h, z], fz_s.at[h, zz], fz_r.at[h, z], zz, c)

    def f_z_in(h, zz):
        return rc(fzs.at[h, zz], fzr.at[h, zz], fz_s.at[h, zz], fz_r.at[h, zz], zz, c)

    def half(which, h):
        rows = pl.ds(pl.multiple_of(which * 256, 256), 256)
        right = d2[:, h * 512:(h + 1) * 512]
        return (dot(xh[rows, 0:256], right) + dot(xl[rows, 0:256], right)).reshape(4, 64, 512)

    for h in range(2):
        fcs[h] = enc(half(1 - core, h))
        f_c(h).start()
    for h in range(2):
        p2[h] = half(core, h)
        f_c(h).wait_recv()
        for yy in ypeer:
            fys[h, yy] = enc(p2[h, yy] + dec(fcr[h, yy]))
            f_y(h, yy).start()
    rows_a, hi, lo = natural()
    lo2 = (rows_a - hi.astype(F32) - lo.astype(F32)).astype(BF)
    back = (lax.broadcasted_iota(jnp.int32, shape_sq, 0) == source_column(lax.broadcasted_iota(jnp.int32, shape_sq, 1))).astype(F32).astype(BF)
    na_ref[...] = dot(hi, back, NT) + dot(lo, back, NT) + dot(lo2, back, NT)
    for h in range(2):
        total = p2[h, y] + dec(fcr[h, y])
        for yy in ypeer:
            f_y_in(h, yy).wait_recv()
            total = total + dec(fyr[h, yy])
        fsum[h] = total.reshape(8, 8, 512)
        for zz in zpeer:
            mine = fsum[h, zz]
            fzs[h, zz] = enc(jnp.concatenate([mine[:, 0:256], mine[:, 256:512]], axis=0))
            f_z(h, zz).start()
    for h in range(2):
        rest = None
        for zz in zpeer:
            f_z_in(h, zz).wait_recv()
            got = dec(fzr[h, zz])
            rest = got if rest is None else rest + got
        gained = fsum[h, z] + jnp.concatenate([rest[0:8], rest[8:16]], axis=1)
        nb_ref[:, h * 512:(h + 1) * 512] = b_own[:, h * 512:(h + 1) * 512] + gained

    for zz in zpeer:
        b_z(zz).wait_send()
        f_2(zz).wait_send()
        t_z(zz).wait_send()
        for h in range(2):
            f_z(h, zz).wait_send()
        for yy in ypeer:
            b_y(yy, zz).wait_send()
    for r in cpeer:
        t_n(r).wait_send()
        f_1(r).wait_send()
        f_3(r).wait_send()
    for yy in ypeer:
        b_y(yy, z).wait_send()
        for h in range(2):
            p_y(h, yy).wait_send()
            n_y(h, yy).wait_send()
            f_y(h, yy).wait_send()
    for yy in ypeer + [y]:
        b_c(yy).wait_send()
        for h in range(2):
            p_c(h, yy).wait_send()
            n_c(h, yy).wait_send()
    for h in range(2):
        f_c(h).wait_send()

    @pl.loop(0, 8)
    def _(s):
        for q in range(4):
            pl.when(jnp.logical_and(s <= z, z < 7))(lambda: x_out(0, s, q, up).wait_send())
            pl.when(jnp.logical_and(s >= z, z > 0))(lambda: x_out(1, s, q, down).wait_send())
            pl.when(s > z)(lambda: z_out(0, s, q, up).wait_send())
            pl.when(s < z)(lambda: z_out(1, s, q, down).wait_send())


def per_device(covariance, weight, factor_a, factor_b):
    n = weight.shape[0]
    vm = pl.BlockSpec(memory_space=pltpu.VMEM)
    blk = (8, C2, 128)
    dma = pltpu.SemaphoreType.DMA
    new_a, new_b = pl.pallas_call(
        kernel,
        name="refine",
        out_shape=(jax.ShapeDtypeStruct((n, C2), F32), jax.ShapeDtypeStruct((8, O), F32)),
        in_specs=[pl.BlockSpec(memory_space=pl.ANY)] * 3 + [vm],
        out_specs=(vm, vm),
        scratch_shapes=[
            pltpu.VMEM((1024, 1024), F32),
            pltpu.VMEM((n, 2, O), BF),
            pltpu.VMEM((n, 2, R), BF),
            pltpu.VMEM((2, n, O), BF),
            pltpu.VMEM((1024, 1024), BF),
            pltpu.VMEM((1024, 1024), BF),
            pltpu.VMEM((1024, 2048), BF),
            pltpu.VMEM((2, 4, 8, 16, 512), BF),
            pltpu.VMEM((C2, O), BF),
            pltpu.VMEM((128, C2), BF),
            pltpu.VMEM(blk, BF),
            pltpu.VMEM((C2, 1024), BF),
            pltpu.VMEM((C2, 1024), BF),
            pltpu.VMEM((8, 64, 128), BF),
            pltpu.VMEM((8, 64, 128), BF),
            pltpu.VMEM((8, 64, 128), BF),
            pltpu.VMEM((8, 64, 128), BF),
            pltpu.VMEM(blk, F32),
            pltpu.VMEM((4, C2, 128), BF),
            pltpu.VMEM((4, C2, 128), BF),
            pltpu.VMEM((4, C2, 128), BF),
            pltpu.VMEM((4, C2, 128), BF),
            pltpu.VMEM((8, 8, 64, 128), BF),
            pltpu.VMEM((8, 64, 128), BF),
            pltpu.VMEM((8, 64, 128), BF),
            pltpu.VMEM(blk, F32),
            pltpu.VMEM((2,) + blk, BF),
            pltpu.VMEM((2,) + blk, BF),
            pltpu.VMEM((256, O), BF),
            pltpu.VMEM((2, 4, 64, 512), F32),
            pltpu.VMEM((2, 4, 64, 512), BF),
            pltpu.VMEM((2, 4, 64, 512), BF),
            pltpu.VMEM((2, 4, 64, 512), BF),
            pltpu.VMEM((2, 4, 64, 512), BF),
            pltpu.VMEM((2, 8, 8, 512), F32),
            pltpu.VMEM((2, 8, 16, 256), BF),
            pltpu.VMEM((2, 8, 16, 256), BF),
            dma, dma, dma,
            dma((8,)), dma((8,)), dma((4, 8)), dma((4, 8)), dma((4,)), dma((4,)),
            dma((8,)), dma((8,)), dma((8,)), dma((8,)), dma((8,)), dma((8,)),
            dma((2, 8, 4)), dma((8, 4)),
            dma((2, 4)), dma((2, 4)), dma((2, 4)), dma((2, 4)),
            dma((2, 4)), dma((2, 4)), dma((2, 8)),
            dma((8,)), dma((8,)), dma((8,)), dma((8,)),
            dma((2, 8, 4)), dma((2, 8, 4)),
            dma((2,)), dma((2,)), dma((2, 4)), dma((2, 4)), dma((2, 8)), dma((2, 8)),
        ],
        compiler_params=pltpu.CompilerParams(
            collective_id=0, has_side_effects=True, vmem_limit_bytes=56 * 2**20
        ),
    )(covariance, weight, factor_a, factor_b)
    return new_a.reshape(n, 2, R), new_b.reshape(2, 4, O)


def solution(mesh):
    in_specs = (
        P(("layer", "row"), "col"),
        P(("layer", "col", "row"), None, None),
        P(("layer", "col", "row"), None, None),
        P("layer", ("row", "col"), None),
    )
    out_specs = (P(("layer", "col", "row"), None, None), P("layer", ("row", "col"), None))
    return jax.shard_map(
        per_device, mesh=mesh, in_specs=in_specs, out_specs=out_specs, check_vma=False
    )
```
